256 devices in a mesh: str: 64 (over y, z, core), ib: 4 (over x).
Axes of the slice: x: 4, y: 4, z: 8, core: 2. Of those that a mesh axis runs over, the one named last changes fastest.
Arguments:
- coeffs: bfloat16 [256, 32768], P('str'), may hold values from -6 to 6
- block_irrep: int32 [256], replicated, may hold values from 0 to 7
- couple_block: int32 [256, 8], replicated, may hold values from 0 to 255
- couple_sign: int32 [256, 8], replicated, may hold values from -1 to 1
- block_order: int32 [256], replicated, may hold values from 0 to 255, each once
- alpha_same: bfloat16 [256, 256], replicated, may hold values from -0.375 to 0.375
- alpha_mixed: bfloat16 [8, 256, 256], P('ib'), may hold values from -0.125 to 0.125
- beta_same: bfloat16 [8, 128, 128], replicated, may hold values from -0.1875 to 0.1875
- beta_mixed: bfloat16 [8, 8, 128, 128], P('ib'), may hold values from -0.1875 to 0.1875
Outputs:
- sigma: bfloat16 [256, 32768], P(None, ('str', 'ib'))
The draws below stay inside these ranges and needn't reach their ends.
Inputs may be any that keep to these rules, and one draw needn't show every extreme that they name: `block_order`: a permutation of the block numbers.
All inputs are finite; a program needn't handle non-finite values.
Results may differ from the reference program's by a relative error of at most 0.0047.
Values may be sent and summed in bfloat16 or wider, within the bound.
A program may use at most 64 MiB of HBM per device.

```python
import jax
import jax.numpy as jnp
from jax import lax

NA = 256
BLK = 128
KC = 8
BPD = 4
NBLK = 256
NB = 32768
NPAIR = 8


def touch_ends(array, own_key, smallest, high):
    index_at = [jax.random.randint(jax.random.fold_in(own_key, axis), (), 0, length) for axis, length in enumerate(array.shape)]
    widest = array.shape.index(max(array.shape))
    beside = index_at[:widest] + [(index_at[widest] + 1) % array.shape[widest]] + index_at[widest + 1:]
    return array.at[tuple(index_at)].set(smallest).at[tuple(beside)].set(high)


def shard_levels(key, extent, pieces, smallest, high):
    def one(dim, parts):
        steps = jax.random.uniform(jax.random.fold_in(jax.random.fold_in(key, 6), dim), (parts,), jnp.float32, smallest / len(pieces), high / len(pieces))
        return jnp.repeat(jnp.exp(steps), extent[dim] // parts).reshape((-1,) + (1,) * (len(extent) - dim - 1))

    gain = one(*pieces[0])
    for cut in pieces[1:]:
        gain = gain * one(*cut)
    return gain


def centred(rng, extent, scale, bound, cuts=(), held_as=jnp.bfloat16):
    result = jax.random.normal(rng, extent, jnp.float32) * scale
    if len(cuts) > 0:
        result = shard_levels(rng, extent, cuts, -0.22, 0.18) * result
    return jnp.clip(result, min=-bound, max=bound).astype(held_as)


def setup_inputs(seed: int = 0) -> dict:
    arg_keys = jax.random.split(jax.random.key(seed), 10)
    coeffs = centred(arg_keys[0], (NA, NB), 1.0, 6.0, ((0, 64),))
    block_irrep = touch_ends(jax.random.randint(arg_keys[1], (NBLK,), 0, 8), jax.random.fold_in(arg_keys[1], 1), 0, 7).astype(jnp.int32)
    couple_block = touch_ends(jax.random.randint(arg_keys[2], (NBLK, KC), 0, NBLK), jax.random.fold_in(arg_keys[2], 1), 0, NBLK - 1).astype(jnp.int32)
    couple_sign = touch_ends(jax.random.randint(arg_keys[3], (NBLK, KC), -1, 2), jax.random.fold_in(arg_keys[3], 1), -1, 1).astype(jnp.int32)
    block_order = jax.random.permutation(arg_keys[4], NBLK).astype(jnp.int32)
    alpha_same = centred(arg_keys[5], (NA, NA), NA ** -0.5, 0.375)
    alpha_mixed = centred(arg_keys[6], (NPAIR, NA, NA), (NA * NPAIR) ** -0.5, 0.125, ((0, 4),))
    beta_same = centred(arg_keys[7], (8, BLK, BLK), (BLK * KC) ** -0.5, 0.1875)
    beta_mixed = centred(arg_keys[8], (NPAIR, 8, BLK, BLK), (BLK * KC) ** -0.5, 0.1875, ((0, 4),))
    return {"coeffs": coeffs, "block_irrep": block_irrep, "couple_block": couple_block, "couple_sign": couple_sign, "block_order": block_order, "alpha_same": alpha_same, "alpha_mixed": alpha_mixed, "beta_same": beta_same, "beta_mixed": beta_mixed}


def reference(coeffs, block_irrep, couple_block, couple_sign, block_order, alpha_same, alpha_mixed, beta_same, beta_mixed):
    block_count = couple_block.shape[0]
    group_count = block_count // BPD
    blocks = coeffs.reshape(NA, block_count, BLK)
    coupled = couple_block[block_order]
    sign_rows = couple_sign[block_order]
    kind_rows = jnp.bitwise_xor(block_irrep[block_order][:, None], block_irrep[coupled])
    kind_weights = jnp.where(kind_rows[:, :, None] == jnp.arange(8, dtype=jnp.int32)[None, None, :], sign_rows[:, :, None], 0).astype(jnp.float32)
    beta_all = jnp.concatenate([beta_same[None], beta_mixed], axis=0).astype(jnp.float32)
    alpha_same_f = alpha_same.astype(jnp.float32)
    alpha_mixed_f = alpha_mixed.astype(jnp.float32)

    def per_group(inputs):
        coupled_part, weight_part, owned = inputs
        picked = blocks[:, coupled_part].astype(jnp.float32)
        grouped = jnp.einsum('ajkc,jkq->ajqc', picked, weight_part).astype(jnp.bfloat16)
        beta_terms = jnp.einsum('ajqc,pqcd->pajd', grouped.astype(jnp.float32), beta_all).astype(jnp.bfloat16).astype(jnp.float32)
        owned_cols = blocks[:, owned].astype(jnp.float32)
        summed = jnp.einsum('ab,bjd->ajd', alpha_same_f, owned_cols) + beta_terms[0]
        summed = summed + jnp.einsum('pab,pbjd->ajd', alpha_mixed_f, beta_terms[1:])
        return summed.astype(jnp.bfloat16)

    result_rows = lax.map(per_group, (coupled.reshape(group_count, BPD, KC), kind_weights.reshape(group_count, BPD, KC, 8), block_order.reshape(group_count, BPD)))
    return jnp.transpose(result_rows, (1, 0, 2, 3)).reshape(NA, NB)
```

```python
import functools

import jax
import jax.numpy as jnp
from jax import lax
from jax.experimental import pallas as pl
from jax.experimental.pallas import tpu as pltpu
from jax.sharding import PartitionSpec as P

MESH = pl.DeviceIdType.MESH
F32 = jnp.float32
BF16 = jnp.bfloat16


def iota(shape, dim):
    return lax.broadcasted_iota(jnp.int32, shape, dim)


def kernel(
    n_str,
    n_ib,
    coef_ref,
    irr_ref,
    cb_ref,
    sg_ref,
    ord_ref,
    as_hbm,
    am_hbm,
    bs_hbm,
    bm_hbm,
    out_ref,
    b_ref,
    a_ref,
    as_ref,
    g_ref,
    z_ref,
    send_a,
    send_b,
    recv_a,
    recv_b,
    part_s,
    part_r,
    load_sem,
    str_send,
    str_recv,
    ib_send,
    ib_recv,
):
    me = lax.axis_index("str")
    ib = lax.axis_index("ib")

    barrier = pltpu.get_barrier_semaphore()

    def greet(k, carry):
        pl.semaphore_signal(
            barrier, inc=1, device_id=(lax.rem(me + k, n_str), ib), device_id_type=MESH
        )
        return carry

    lax.fori_loop(1, n_str, greet, 0)
    for k in range(1, n_ib):
        pl.semaphore_signal(
            barrier, inc=1, device_id=(me, lax.rem(ib + k, n_ib)), device_id_type=MESH
        )

    loads = [
        pltpu.make_async_copy(bm_hbm.at[0], b_ref.at[:, pl.ds(0, 128)], load_sem.at[0]),
        pltpu.make_async_copy(bm_hbm.at[1], b_ref.at[:, pl.ds(128, 128)], load_sem.at[1]),
        pltpu.make_async_copy(bs_hbm, b_ref.at[:, pl.ds(256, 128)], load_sem.at[2]),
        pltpu.make_async_copy(am_hbm.at[0], a_ref.at[:, pl.ds(0, 256)], load_sem.at[3]),
        pltpu.make_async_copy(am_hbm.at[1], a_ref.at[:, pl.ds(256, 256)], load_sem.at[4]),
        pltpu.make_async_copy(as_hbm, as_ref, load_sem.at[5]),
    ]
    for load in loads:
        load.start()

    cb = cb_ref[...]
    sg = sg_ref[...]
    row = iota((256, 256), 0)
    counts = jnp.zeros((256, 256), jnp.int32)
    for k in range(8):
        counts = counts + jnp.where(row == cb[k : k + 1, :], sg[k : k + 1, :], 0)
    counts = counts.astype(F32).astype(BF16)
    irr = irr_ref[...]
    irr_f = irr.astype(F32)
    order_f = ord_ref[...].astype(F32)
    lane = iota((64, 256), 1)
    sub = iota((64, 256), 0)
    lane_f = lane.astype(F32)
    coef = coef_ref[...]

    r = iota((512, 512), 0)
    c = iota((512, 512), 1)
    to_msg = jnp.where(
        c == (r // 4 % 2) * 256 + (r % 4) * 64 + r // 8, 1.0, 0.0
    ).astype(BF16)

    def unit(t, slot, last):
        place = lax.rem(ib + t, n_ib)
        owned = jnp.sum(
            jnp.where(lane == 4 * sub + place, order_f, 0.0), axis=1, keepdims=True
        )
        pick = lane_f == owned
        irr_row = jnp.sum(jnp.where(pick, irr_f, 0.0), axis=1, keepdims=True).astype(jnp.int32)
        pick = jnp.where(pick, 1.0, 0.0).astype(BF16)
        near = lax.dot_general(
            pick, counts, (((1,), (1,)), ((), ())), preferred_element_type=F32
        )
        kind = jnp.bitwise_xor(irr_row, irr)
        weights = jnp.concatenate(
            [jnp.where(kind == q, near, 0.0) for q in range(8)], axis=0
        ).astype(BF16)
        grouped = jnp.dot(weights, coef, preferred_element_type=F32).astype(BF16)
        for q in range(8):
            for a in range(4):
                g_ref[a * 64 : (a + 1) * 64, q * 128 : (q + 1) * 128] = grouped[
                    q * 64 : (q + 1) * 64, a * 128 : (a + 1) * 128
                ]
        at = pl.ds(slot * 128, 128)
        cols = 384 if last else 256
        mixed = jnp.dot(g_ref[...], b_ref[:, :cols], preferred_element_type=F32).astype(BF16)
        z_ref[0:256, at] = mixed[:, 0:128]
        z_ref[256:512, at] = mixed[:, 128:256]
        if last:
            at = pl.ds(slot * 128 + 128, 128)
            own = jnp.dot(pick, coef, preferred_element_type=F32).astype(BF16)
            for a in range(4):
                z_ref[a * 64 : (a + 1) * 64, at] = own[:, a * 128 : (a + 1) * 128]
            z_ref[256:512, at] = mixed[:, 256:384]

    def pack(lo, width):
        rows = jnp.dot(to_msg, z_ref[:, lo : lo + width], preferred_element_type=F32)
        return rows.reshape(64, 8, width).astype(BF16)

    def send_all(src, dst, which):
        def one(k, carry):
            to = lax.rem(me + k, n_str)
            pltpu.make_async_remote_copy(
                src_ref=src.at[to],
                dst_ref=dst.at[me],
                send_sem=str_send.at[which],
                recv_sem=str_recv.at[which],
                device_id=(to, ib),
                device_id_type=MESH,
            ).start()
            return carry

        lax.fori_loop(1, n_str, one, 0)

    def await_all(ref, sem):
        some = ref.at[pl.ds(0, n_str - 1)]
        pltpu.make_async_copy(some, some, sem).wait()

    for load in loads[:3]:
        load.wait()
    for t in range(1, 4):
        unit(t, t - 1, False)
    send_a[...] = pack(0, 384)
    pl.semaphore_wait(barrier, n_str - 1 + n_ib - 1)
    send_all(send_a, recv_a, 0)
    unit(0, 3, True)
    send_b[...] = pack(384, 256)
    send_all(send_b, recv_b, 1)

    recv_a[me] = send_a[me]
    recv_b[me] = send_b[me]
    from_cols = jnp.where(
        r == (c // 4 % 2) * 256 + (c // 8) * 4 + c % 4, 1.0, 0.0
    ).astype(BF16)
    for load in loads[3:]:
        load.wait()
    alpha = jnp.dot(a_ref[...], from_cols, preferred_element_type=F32).astype(BF16)
    eye = jnp.where(iota((256, 256), 0) == iota((256, 256), 1), 1.0, 0.0).astype(BF16)
    same = jnp.concatenate([as_ref[...], eye], axis=1)
    same = jnp.dot(same, from_cols, preferred_element_type=F32).astype(BF16)

    def received(ref):
        x = ref[...].astype(F32)
        return x.reshape(512, x.shape[2]).astype(BF16)

    await_all(recv_a, str_recv.at[0])
    partial = jnp.dot(alpha, received(recv_a), preferred_element_type=F32).astype(BF16)
    copies = []
    for u in range(3):
        part_s[u] = partial[:, u * 128 : (u + 1) * 128]
        copy = pltpu.make_async_remote_copy(
            src_ref=part_s.at[u],
            dst_ref=part_r.at[u],
            send_sem=ib_send.at[u],
            recv_sem=ib_recv.at[u],
            device_id=(me, lax.rem(ib + 1 + u, n_ib)),
            device_id_type=MESH,
        )
        copy.start()
        copies.append(copy)
    await_all(recv_b, str_recv.at[1])
    x = received(recv_b)
    total = jnp.dot(alpha, x[:, 0:128], preferred_element_type=F32) + jnp.dot(
        same, x[:, 128:256], preferred_element_type=F32
    )
    for u in range(3):
        copies[u].wait_recv()
        total = total + part_r[u].astype(F32)
    out_ref[...] = total.astype(BF16)
    for u in range(3):
        copies[u].wait_send()
    await_all(send_a, str_send.at[0])
    await_all(send_b, str_send.at[1])


def local(
    n_str,
    n_ib,
    coeffs,
    block_irrep,
    couple_block,
    couple_sign,
    block_order,
    alpha_same,
    alpha_mixed,
    beta_same,
    beta_mixed,
):
    coef = coeffs.reshape(4, 256, 128).transpose(1, 0, 2).reshape(256, 512)
    vmem = pl.BlockSpec(memory_space=pltpu.VMEM)
    any_ = pl.BlockSpec(memory_space=pl.ANY)
    return pl.pallas_call(
        functools.partial(kernel, n_str, n_ib),
        out_shape=jax.ShapeDtypeStruct((256, 128), BF16),
        in_specs=[vmem] * 5 + [any_] * 4,
        out_specs=vmem,
        scratch_shapes=[
            pltpu.VMEM((1024, 384), BF16),
            pltpu.VMEM((256, 512), BF16),
            pltpu.VMEM((256, 256), BF16),
            pltpu.VMEM((256, 1024), BF16),
            pltpu.VMEM((512, 640), BF16),
            pltpu.VMEM((64, 8, 384), BF16),
            pltpu.VMEM((64, 8, 256), BF16),
            pltpu.VMEM((64, 8, 384), BF16),
            pltpu.VMEM((64, 8, 256), BF16),
            pltpu.VMEM((3, 256, 128), BF16),
            pltpu.VMEM((3, 256, 128), BF16),
            pltpu.SemaphoreType.DMA((6,)),
            pltpu.SemaphoreType.DMA((2,)),
            pltpu.SemaphoreType.DMA((2,)),
            pltpu.SemaphoreType.DMA((3,)),
            pltpu.SemaphoreType.DMA((3,)),
        ],
        compiler_params=pltpu.CompilerParams(
            collective_id=0, has_side_effects=True, vmem_limit_bytes=48 * 1024 * 1024
        ),
    )(
        coef,
        block_irrep.reshape(1, 256),
        couple_block.T,
        couple_sign.T,
        block_order.reshape(1, 256),
        alpha_same,
        alpha_mixed,
        beta_same.reshape(1024, 128),
        beta_mixed.reshape(2, 1024, 128),
    )


def solution(mesh):
    in_specs = (
        P("str", None),
        P(),
        P(),
        P(),
        P(),
        P(),
        P("ib", None, None),
        P(),
        P("ib", None, None, None),
    )
    body = functools.partial(local, mesh.shape["str"], mesh.shape["ib"])
    return jax.shard_map(
        body, mesh=mesh, in_specs=in_specs, out_specs=P(None, ("str", "ib")), check_vma=False
    )
```

```python
import functools

import jax
import jax.numpy as jnp
from jax import lax
from jax.experimental import pallas as pl
from jax.experimental.pallas import tpu as pltpu
from jax.sharding import PartitionSpec as P

MESH = pl.DeviceIdType.MESH
F32 = jnp.float32
BF16 = jnp.bfloat16


def iota(shape, dim):
    return lax.broadcasted_iota(jnp.int32, shape, dim)


def kernel(
    n_str,
    n_ib,
    coef_hbm,
    irr_hbm,
    cb_hbm,
    sg_hbm,
    ord_hbm,
    as_hbm,
    am_hbm,
    bs_hbm,
    bm_hbm,
    out_ref,
    coef_ref,
    coef_f,
    c_ref,
    irr_ref,
    cb_ref,
    sg_ref,
    ord_ref,
    b_ref,
    a_ref,
    as_ref,
    g_ref,
    z_ref,
    send_a,
    send_b,
    recv_a,
    recv_b,
    part_s,
    part_r,
    load_sem,
    str_send,
    str_recv,
    ib_send,
    ib_recv,
):
    me = lax.axis_index("str")
    ib = lax.axis_index("ib")

    loads = [
        pltpu.make_async_copy(cb_hbm, cb_ref, load_sem.at[0]),
        pltpu.make_async_copy(sg_hbm, sg_ref, load_sem.at[1]),
        pltpu.make_async_copy(irr_hbm, irr_ref, load_sem.at[2]),
        pltpu.make_async_copy(ord_hbm, ord_ref, load_sem.at[3]),
        pltpu.make_async_copy(coef_hbm, coef_ref, load_sem.at[4]),
        pltpu.make_async_copy(bm_hbm.at[0], b_ref.at[:, pl.ds(0, 128)], load_sem.at[5]),
        pltpu.make_async_copy(bm_hbm.at[1], b_ref.at[:, pl.ds(128, 128)], load_sem.at[6]),
        pltpu.make_async_copy(bs_hbm, b_ref.at[:, pl.ds(256, 128)], load_sem.at[7]),
        pltpu.make_async_copy(am_hbm.at[0], a_ref.at[:, pl.ds(0, 256)], load_sem.at[8]),
        pltpu.make_async_copy(am_hbm.at[1], a_ref.at[:, pl.ds(256, 256)], load_sem.at[9]),
        pltpu.make_async_copy(as_hbm, as_ref, load_sem.at[10]),
    ]
    for load in loads:
        load.start()

    barrier = pltpu.get_barrier_semaphore()

    def greet(k, carry):
        pl.semaphore_signal(
            barrier, inc=1, device_id=(lax.rem(me + k, n_str), ib), device_id_type=MESH
        )
        return carry

    lax.fori_loop(1, n_str, greet, 0)
    for k in range(1, n_ib):
        pl.semaphore_signal(
            barrier, inc=1, device_id=(me, lax.rem(ib + k, n_ib)), device_id_type=MESH
        )

    r = iota((512, 512), 0)
    c = iota((512, 512), 1)
    for load in loads[:8]:
        load.wait()
    coef_f[...] = coef_ref[...].astype(F32)
    for a in range(4):
        c_ref[:, a * 128 : (a + 1) * 128] = coef_f[:, a, :].astype(BF16)

    cb = cb_ref[...]
    sg = sg_ref[...]
    row = iota((256, 256), 0)
    counts = jnp.zeros((256, 256), jnp.int32)
    for k in range(8):
        counts = counts + jnp.where(row == cb[k : k + 1, :], sg[k : k + 1, :], 0)
    counts = counts.astype(F32).astype(BF16)
    irr = irr_ref[...]
    irr_f = irr.astype(F32)
    order_f = ord_ref[...].astype(F32)
    lane = iota((64, 256), 1)
    sub = iota((64, 256), 0)
    lane_f = lane.astype(F32)

    to_msg = jnp.where(
        c == (r // 4 % 2) * 256 + (r % 4) * 64 + r // 8, 1.0, 0.0
    ).astype(BF16)

    def unit(t, slot, last):
        place = lax.rem(ib + t, n_ib)
        owned = jnp.sum(
            jnp.where(lane == 4 * sub + place, order_f, 0.0), axis=1, keepdims=True
        )
        pick = lane_f == owned
        irr_row = jnp.sum(jnp.where(pick, irr_f, 0.0), axis=1, keepdims=True).astype(jnp.int32)
        pick = jnp.where(pick, 1.0, 0.0).astype(BF16)
        near = lax.dot_general(
            pick, counts, (((1,), (1,)), ((), ())), preferred_element_type=F32
        )
        kind = jnp.bitwise_xor(irr_row, irr)
        weights = jnp.concatenate(
            [jnp.where(kind == q, near, 0.0) for q in range(8)], axis=0
        ).astype(BF16)
        grouped = jnp.dot(weights, c_ref[...], preferred_element_type=F32).astype(BF16)
        for q in range(8):
            for a in range(4):
                g_ref[a * 64 : (a + 1) * 64, q * 128 : (q + 1) * 128] = grouped[
                    q * 64 : (q + 1) * 64, a * 128 : (a + 1) * 128
                ]
        at = pl.ds(slot * 128, 128)
        cols = 384 if last else 256
        mixed = jnp.dot(g_ref[...], b_ref[:, :cols], preferred_element_type=F32).astype(BF16)
        z_ref[0:256, at] = mixed[:, 0:128]
        z_ref[256:512, at] = mixed[:, 128:256]
        if last:
            at = pl.ds(slot * 128 + 128, 128)
            own = jnp.dot(pick, c_ref[...], preferred_element_type=F32).astype(BF16)
            for a in range(4):
                z_ref[a * 64 : (a + 1) * 64, at] = own[:, a * 128 : (a + 1) * 128]
            z_ref[256:512, at] = mixed[:, 256:384]

    def pack(lo, width):
        rows = jnp.dot(to_msg, z_ref[:, lo : lo + width], preferred_element_type=F32)
        return rows.reshape(64, 8, width).astype(BF16)

    def send_all(src, dst, which):
        def one(k, carry):
            to = lax.rem(me + k, n_str)
            pltpu.make_async_remote_copy(
                src_ref=src.at[to],
                dst_ref=dst.at[me],
                send_sem=str_send.at[which],
                recv_sem=str_recv.at[which],
                device_id=(to, ib),
                device_id_type=MESH,
            ).start()
            return carry

        lax.fori_loop(1, n_str, one, 0)

    def await_all(ref, sem):
        some = ref.at[pl.ds(0, n_str - 1)]
        pltpu.make_async_copy(some, some, sem).wait()

    for t in range(1, 4):
        unit(t, t - 1, False)
    send_a[...] = pack(0, 384)
    pl.semaphore_wait(barrier, n_str - 1 + n_ib - 1)
    send_all(send_a, recv_a, 0)
    unit(0, 3, True)
    send_b[...] = pack(384, 256)
    send_all(send_b, recv_b, 1)

    for load in loads[8:]:
        load.wait()
    recv_a[me] = send_a[me]
    recv_b[me] = send_b[me]
    from_cols = jnp.where(
        r == (c // 4 % 2) * 256 + (c // 8) * 4 + c % 4, 1.0, 0.0
    ).astype(BF16)
    alpha = jnp.dot(a_ref[...], from_cols, preferred_element_type=F32).astype(BF16)
    eye = jnp.where(iota((256, 256), 0) == iota((256, 256), 1), 1.0, 0.0).astype(BF16)
    same = jnp.concatenate([as_ref[...], eye], axis=1)
    same = jnp.dot(same, from_cols, preferred_element_type=F32).astype(BF16)

    def received(ref):
        x = ref[...].astype(F32)
        return x.reshape(512, x.shape[2]).astype(BF16)

    await_all(recv_a, str_recv.at[0])
    partial = jnp.dot(alpha, received(recv_a), preferred_element_type=F32).astype(BF16)
    copies = []
    for u in range(3):
        part_s[u] = partial[:, u * 128 : (u + 1) * 128]
        copy = pltpu.make_async_remote_copy(
            src_ref=part_s.at[u],
            dst_ref=part_r.at[u],
            send_sem=ib_send.at[u],
            recv_sem=ib_recv.at[u],
            device_id=(me, lax.rem(ib + 1 + u, n_ib)),
            device_id_type=MESH,
        )
        copy.start()
        copies.append(copy)
    await_all(recv_b, str_recv.at[1])
    x = received(recv_b)
    total = jnp.dot(alpha, x[:, 0:128], preferred_element_type=F32) + jnp.dot(
        same, x[:, 128:256], preferred_element_type=F32
    )
    for u in range(3):
        copies[u].wait_recv()
        total = total + part_r[u].astype(F32)
    out_ref[...] = total.astype(BF16)
    for u in range(3):
        copies[u].wait_send()
    await_all(send_a, str_send.at[0])
    await_all(send_b, str_send.at[1])


def local(
    n_str,
    n_ib,
    coeffs,
    block_irrep,
    couple_block,
    couple_sign,
    block_order,
    alpha_same,
    alpha_mixed,
    beta_same,
    beta_mixed,
):
    hbm = pl.BlockSpec(memory_space=pltpu.HBM)
    return pl.pallas_call(
        functools.partial(kernel, n_str, n_ib),
        out_shape=jax.ShapeDtypeStruct((256, 128), BF16),
        in_specs=[hbm] * 9,
        out_specs=pl.BlockSpec(memory_space=pltpu.VMEM),
        scratch_shapes=[
            pltpu.VMEM((256, 4, 128), BF16),
            pltpu.VMEM((256, 4, 128), F32),
            pltpu.VMEM((256, 512), BF16),
            pltpu.VMEM((1, 256), jnp.int32),
            pltpu.VMEM((8, 256), jnp.int32),
            pltpu.VMEM((8, 256), jnp.int32),
            pltpu.VMEM((1, 256), jnp.int32),
            pltpu.VMEM((1024, 384), BF16),
            pltpu.VMEM((256, 512), BF16),
            pltpu.VMEM((256, 256), BF16),
            pltpu.VMEM((256, 1024), BF16),
            pltpu.VMEM((512, 640), BF16),
            pltpu.VMEM((64, 8, 384), BF16),
            pltpu.VMEM((64, 8, 256), BF16),
            pltpu.VMEM((64, 8, 384), BF16),
            pltpu.VMEM((64, 8, 256), BF16),
            pltpu.VMEM((3, 256, 128), BF16),
            pltpu.VMEM((3, 256, 128), BF16),
            pltpu.SemaphoreType.DMA((11,)),
            pltpu.SemaphoreType.DMA((2,)),
            pltpu.SemaphoreType.DMA((2,)),
            pltpu.SemaphoreType.DMA((3,)),
            pltpu.SemaphoreType.DMA((3,)),
        ],
        compiler_params=pltpu.CompilerParams(
            collective_id=0, has_side_effects=True, vmem_limit_bytes=62 * 1024 * 1024
        ),
    )(
        coeffs.reshape(4, 256, 128).transpose(1, 0, 2),
        block_irrep.reshape(1, 256),
        couple_block.T,
        couple_sign.T,
        block_order.reshape(1, 256),
        alpha_same,
        alpha_mixed,
        beta_same.reshape(1024, 128),
        beta_mixed.reshape(2, 1024, 128),
    )


def solution(mesh):
    in_specs = (
        P("str", None),
        P(),
        P(),
        P(),
        P(),
        P(),
        P("ib", None, None),
        P(),
        P("ib", None, None, None),
    )
    body = functools.partial(local, mesh.shape["str"], mesh.shape["ib"])
    return jax.shard_map(
        body, mesh=mesh, in_specs=in_specs, out_specs=P(None, ("str", "ib")), check_vma=False
    )
```

```python
import functools

import jax
import jax.numpy as jnp
from jax import lax
from jax.experimental import pallas as pl
from jax.experimental.pallas import tpu as pltpu
from jax.sharding import PartitionSpec as P

MESH = pl.DeviceIdType.MESH
F32 = jnp.float32
BF16 = jnp.bfloat16


def iota(shape, dim):
    return lax.broadcasted_iota(jnp.int32, shape, dim)


def kernel(
    n_str,
    n_ib,
    coef_hbm,
    irr_hbm,
    cb_hbm,
    sg_hbm,
    ord_hbm,
    as_hbm,
    am_hbm,
    bs_hbm,
    bm_hbm,
    out_ref,
    coef_ref,
    coef_f,
    c_ref,
    irr_ref,
    cb_ref,
    sg_ref,
    ord_ref,
    b_ref,
    a_ref,
    as_ref,
    msg_ref,
    g_ref,
    z_ref,
    send_a,
    send_b,
    recv_a,
    recv_b,
    part_s,
    part_r,
    load_sem,
    str_send,
    str_recv,
    ib_send,
    ib_recv,
    late_sem,
    plane_sem,
    all_sem,
):
    me = lax.axis_index("str")
    ib = lax.axis_index("ib")

    loads = [
        pltpu.make_async_copy(cb_hbm, cb_ref, load_sem.at[0]),
        pltpu.make_async_copy(sg_hbm, sg_ref, load_sem.at[1]),
        pltpu.make_async_copy(irr_hbm, irr_ref, load_sem.at[2]),
        pltpu.make_async_copy(ord_hbm, ord_ref, load_sem.at[3]),
        pltpu.make_async_copy(coef_hbm, coef_ref, load_sem.at[4]),
        pltpu.make_async_copy(bm_hbm.at[0], b_ref.at[:, pl.ds(0, 128)], load_sem.at[5]),
        pltpu.make_async_copy(bm_hbm.at[1], b_ref.at[:, pl.ds(128, 128)], load_sem.at[6]),
        pltpu.make_async_copy(bs_hbm, b_ref.at[:, pl.ds(256, 128)], load_sem.at[7]),
        pltpu.make_async_copy(am_hbm.at[0], a_ref.at[:, pl.ds(0, 256)], load_sem.at[8]),
        pltpu.make_async_copy(am_hbm.at[1], a_ref.at[:, pl.ds(256, 256)], load_sem.at[9]),
        pltpu.make_async_copy(as_hbm, as_ref, load_sem.at[10]),
    ]
    for load in loads:
        load.start()

    y, z, core = me // 16, (me // 2) % 8, me % 2
    late = z >= 4

    def place(y_to, z_to, core_to):
        return (((y_to % 4) * 8) + (z_to % 8)) * 2 + core_to % 2

    barrier = pltpu.get_barrier_semaphore()

    def say(sem, y_to, z_to, core_to):
        pl.semaphore_signal(
            sem, inc=1, device_id=(place(y_to, z_to, core_to), ib), device_id_type=MESH
        )

    for k in range(1, n_ib):
        pl.semaphore_signal(
            barrier, inc=1, device_id=(me, lax.rem(ib + k, n_ib)), device_id_type=MESH
        )

    for k in range(1, 64):
        pl.semaphore_signal(
            barrier, inc=1, device_id=((me + k) % 64, ib), device_id_type=MESH
        )

    r = iota((256, 256), 0)
    c = iota((256, 256), 1)
    msg_ref[...] = jnp.where(
        c == (r // 4 % 2) * 128 + (r % 4) * 32 + r // 8, 1.0, 0.0
    ).astype(BF16)
    lane = iota((32, 256), 1)
    sub = iota((32, 256), 0)
    lane_f = lane.astype(F32)
    row = iota((256, 256), 0)

    for load in loads[:4]:
        load.wait()
    cb = cb_ref[...]
    sg = sg_ref[...]
    counts = jnp.zeros((256, 256), jnp.int32)
    for k in range(8):
        counts = counts + jnp.where(row == cb[k : k + 1, :], sg[k : k + 1, :], 0)
    counts = counts.astype(F32).astype(BF16)
    irr = irr_ref[...]
    irr_f = irr.astype(F32)
    order_f = ord_ref[...].astype(F32)

    loads[4].wait()
    coef_f[...] = coef_ref[...].astype(F32)
    for a in range(4):
        c_ref[:, a * 128 : (a + 1) * 128] = coef_f[:, a, :].astype(BF16)
    for load in loads[5:8]:
        load.wait()

    def choose(t, half):
        owner = (sub // 8) * 16 + (4 * half + sub // 2 % 4) * 2 + sub % 2
        position = lax.rem(ib + t, n_ib)
        owned = jnp.sum(
            jnp.where(lane == 4 * owner + position, order_f, 0.0), axis=1, keepdims=True
        )
        return jnp.where(lane_f == owned, 1.0, 0.0)

    def units(ts, half, cols):
        n = len(ts)
        pick = jnp.concatenate([choose(t, half) for t in ts], axis=0)
        irr_row = jnp.sum(pick * irr_f, axis=1, keepdims=True).astype(jnp.int32)
        pick = pick.astype(BF16)
        near = lax.dot_general(
            pick, counts, (((1,), (1,)), ((), ())), preferred_element_type=F32
        )
        kind = jnp.bitwise_xor(irr_row, irr)
        weights = jnp.concatenate(
            [jnp.where(kind == q, near, 0.0).astype(BF16) for q in range(8)], axis=0
        )
        grouped = jnp.dot(weights, c_ref[...], preferred_element_type=F32).astype(BF16)
        for q in range(8):
            for u in range(n):
                for a in range(4):
                    g_ref[u * 128 + a * 32 : u * 128 + (a + 1) * 32, q * 128 : (q + 1) * 128] = (
                        grouped[q * n * 32 + u * 32 : q * n * 32 + (u + 1) * 32, a * 128 : (a + 1) * 128]
                    )
        mixed = jnp.dot(
            g_ref[: n * 128, :], b_ref[:, :cols], preferred_element_type=F32
        ).astype(BF16)
        for u in range(n):
            z_ref[0:128, u * 128 : (u + 1) * 128] = mixed[u * 128 : (u + 1) * 128, 0:128]
            z_ref[128:256, u * 128 : (u + 1) * 128] = mixed[u * 128 : (u + 1) * 128, 128:256]
        return pick, mixed

    def pack(width):
        rows = jnp.dot(msg_ref[...], z_ref[:, :width], preferred_element_type=F32)
        return rows.reshape(32, 8, width).astype(BF16)

    def chunk_a(half):
        units((1, 2, 3), half, 256)
        send_a[half * 32 : (half + 1) * 32] = pack(384)

    def chunk_b(half):
        pick, mixed = units((0,), half, 384)
        own = jnp.dot(pick, c_ref[...], preferred_element_type=F32).astype(BF16)
        for a in range(4):
            z_ref[a * 32 : (a + 1) * 32, 128:256] = own[:, a * 128 : (a + 1) * 128]
        z_ref[128:256, 128:256] = mixed[:, 256:384]
        send_b[half * 32 : (half + 1) * 32] = pack(256)

    sends = ((send_a, recv_a), (send_b, recv_b))

    def send(which, z_to):
        src, dst = sends[which]

        def one(k, carry):
            y_to, core_to = (y + k // 2) % 4, (core + k) % 2
            to = place(y_to, z_to, core_to)
            pltpu.make_async_remote_copy(
                src_ref=src.at[(z_to // 4) * 32 + y_to * 8 + (z_to % 4) * 2 + core_to],
                dst_ref=dst.at[me],
                send_sem=str_send.at[which],
                recv_sem=str_recv.at[which],
                device_id=(to, ib),
                device_id_type=MESH,
            ).start()
            return carry

        lax.fori_loop(jnp.where(z == z_to, 1, 0), 8, one, 0)

    def await_all(ref, sem):
        some = ref.at[pl.ds(0, n_str - 1)]
        pltpu.make_async_copy(some, some, sem).wait()

    chunk_a(0)
    pl.semaphore_wait(barrier, 63 + n_ib - 1)
    send(0, 0)
    send(0, 1)
    send(0, 2)
    send(0, 3)
    chunk_a(1)
    send(0, 7)
    send(0, 4)
    send(0, 6)
    send(0, 5)
    chunk_b(0)
    send(1, 0)
    send(1, 1)
    send(1, 2)
    send(1, 3)
    chunk_b(1)
    send(1, 7)
    send(1, 4)
    send(1, 6)
    send(1, 5)
    mine = (z // 4) * 32 + y * 8 + (z % 4) * 2 + core
    recv_a[me] = send_a[mine]
    recv_b[me] = send_b[mine]
    r = iota((512, 512), 0)
    c = iota((512, 512), 1)
    from_cols = jnp.where(
        r == (c // 4 % 2) * 256 + (c // 8) * 4 + c % 4, 1.0, 0.0
    ).astype(BF16)
    for load in loads[8:]:
        load.wait()
    alpha = jnp.dot(a_ref[...], from_cols, preferred_element_type=F32).astype(BF16)
    eye = jnp.where(iota((256, 256), 0) == iota((256, 256), 1), 1.0, 0.0).astype(BF16)
    same = jnp.concatenate([as_ref[...], eye], axis=1)
    same = jnp.dot(same, from_cols, preferred_element_type=F32).astype(BF16)

    def received(ref):
        x = ref[...].astype(F32)
        return x.reshape(512, x.shape[2]).astype(BF16)

    await_all(recv_a, str_recv.at[0])
    partial = jnp.dot(alpha, received(recv_a), preferred_element_type=F32).astype(BF16)
    for u in range(3):
        part_s[u] = partial[:, u * 128 : (u + 1) * 128]

    def to_ib(u, ib_to):
        return pltpu.make_async_remote_copy(
            src_ref=part_s.at[u],
            dst_ref=part_r.at[u],
            send_sem=ib_send.at[u],
            recv_sem=ib_recv.at[u],
            device_id=(me, ib_to),
            device_id_type=MESH,
        )

    for ib_to in range(n_ib):

        @pl.when(ib_to != ib)
        def _():
            to_ib(lax.rem(ib_to - ib + n_ib - 1, n_ib), ib_to).start()

    copies = [to_ib(u, lax.rem(ib + 1 + u, n_ib)) for u in range(3)]
    await_all(recv_b, str_recv.at[1])
    x = received(recv_b)
    total = jnp.dot(alpha, x[:, 0:128], preferred_element_type=F32) + jnp.dot(
        same, x[:, 128:256], preferred_element_type=F32
    )
    for u in range(3):
        copies[u].wait_recv()
        total = total + part_r[u].astype(F32)
    out_ref[...] = total.astype(BF16)
    for u in range(3):
        copies[u].wait_send()
    await_all(send_a, str_send.at[0])
    await_all(send_b, str_send.at[1])


def local(
    n_str,
    n_ib,
    coeffs,
    block_irrep,
    couple_block,
    couple_sign,
    block_order,
    alpha_same,
    alpha_mixed,
    beta_same,
    beta_mixed,
):
    hbm = pl.BlockSpec(memory_space=pltpu.HBM)
    return pl.pallas_call(
        functools.partial(kernel, n_str, n_ib),
        out_shape=jax.ShapeDtypeStruct((256, 128), BF16),
        in_specs=[hbm] * 9,
        out_specs=pl.BlockSpec(memory_space=pltpu.VMEM),
        scratch_shapes=[
            pltpu.VMEM((256, 4, 128), BF16),
            pltpu.VMEM((256, 4, 128), F32),
            pltpu.VMEM((256, 512), BF16),
            pltpu.VMEM((1, 256), jnp.int32),
            pltpu.VMEM((8, 256), jnp.int32),
            pltpu.VMEM((8, 256), jnp.int32),
            pltpu.VMEM((1, 256), jnp.int32),
            pltpu.VMEM((1024, 384), BF16),
            pltpu.VMEM((256, 512), BF16),
            pltpu.VMEM((256, 256), BF16),
            pltpu.VMEM((256, 256), BF16),
            pltpu.VMEM((384, 1024), BF16),
            pltpu.VMEM((256, 384), BF16),
            pltpu.VMEM((64, 8, 384), BF16),
            pltpu.VMEM((64, 8, 256), BF16),
            pltpu.VMEM((64, 8, 384), BF16),
            pltpu.VMEM((64, 8, 256), BF16),
            pltpu.VMEM((3, 256, 128), BF16),
            pltpu.VMEM((3, 256, 128), BF16),
            pltpu.SemaphoreType.DMA((11,)),
            pltpu.SemaphoreType.DMA((2,)),
            pltpu.SemaphoreType.DMA((2,)),
            pltpu.SemaphoreType.DMA((3,)),
            pltpu.SemaphoreType.DMA((3,)),
            pltpu.SemaphoreType.REGULAR,
            pltpu.SemaphoreType.REGULAR,
            pltpu.SemaphoreType.REGULAR,
        ],
        compiler_params=pltpu.CompilerParams(
            collective_id=0, has_side_effects=True, vmem_limit_bytes=62 * 1024 * 1024
        ),
    )(
        coeffs.reshape(4, 256, 128).transpose(1, 0, 2),
        block_irrep.reshape(1, 256),
        couple_block.T,
        couple_sign.T,
        block_order.reshape(1, 256),
        alpha_same,
        alpha_mixed,
        beta_same.reshape(1024, 128),
        beta_mixed.reshape(2, 1024, 128),
    )


def solution(mesh):
    in_specs = (
        P("str", None),
        P(),
        P(),
        P(),
        P(),
        P(),
        P("ib", None, None),
        P(),
        P("ib", None, None, None),
    )
    body = functools.partial(local, mesh.shape["str"], mesh.shape["ib"])
    return jax.shard_map(
        body, mesh=mesh, in_specs=in_specs, out_specs=P(None, ("str", "ib")), check_vma=False
    )
```

```python
import functools

import jax
import jax.numpy as jnp
from jax import lax
from jax.experimental import pallas as pl
from jax.experimental.pallas import tpu as pltpu
from jax.sharding import PartitionSpec as P

MESH = pl.DeviceIdType.MESH
F32 = jnp.float32
BF16 = jnp.bfloat16


def iota(shape, dim):
    return lax.broadcasted_iota(jnp.int32, shape, dim)


def kernel(
    n_str,
    n_ib,
    coef_hbm,
    irr_hbm,
    cb_hbm,
    sg_hbm,
    ord_hbm,
    as_hbm,
    am_hbm,
    bs_hbm,
    bm_hbm,
    out_ref,
    coef_ref,
    coef_f,
    c_ref,
    irr_ref,
    cb_ref,
    sg_ref,
    ord_ref,
    b_ref,
    a_ref,
    as_ref,
    msg_ref,
    g_ref,
    z_ref,
    send_a,
    send_b,
    recv_a,
    recv_b,
    part_s,
    part_r,
    load_sem,
    str_send,
    str_recv,
    ib_send,
    ib_recv,
    late_sem,
    plane_sem,
    all_sem,
):
    me = lax.axis_index("str")
    ib = lax.axis_index("ib")

    loads = [
        pltpu.make_async_copy(cb_hbm, cb_ref, load_sem.at[0]),
        pltpu.make_async_copy(sg_hbm, sg_ref, load_sem.at[1]),
        pltpu.make_async_copy(irr_hbm, irr_ref, load_sem.at[2]),
        pltpu.make_async_copy(ord_hbm, ord_ref, load_sem.at[3]),
        pltpu.make_async_copy(coef_hbm, coef_ref, load_sem.at[4]),
        pltpu.make_async_copy(bm_hbm.at[0], b_ref.at[:, pl.ds(0, 128)], load_sem.at[5]),
        pltpu.make_async_copy(bm_hbm.at[1], b_ref.at[:, pl.ds(128, 128)], load_sem.at[6]),
        pltpu.make_async_copy(bs_hbm, b_ref.at[:, pl.ds(256, 128)], load_sem.at[7]),
        pltpu.make_async_copy(am_hbm.at[0], a_ref.at[:, pl.ds(0, 256)], load_sem.at[8]),
        pltpu.make_async_copy(am_hbm.at[1], a_ref.at[:, pl.ds(256, 256)], load_sem.at[9]),
        pltpu.make_async_copy(as_hbm, as_ref, load_sem.at[10]),
    ]
    for load in loads:
        load.start()

    y, z, core = me // 16, (me // 2) % 8, me % 2
    late = z >= 4

    def place(y_to, z_to, core_to):
        return (((y_to % 4) * 8) + (z_to % 8)) * 2 + core_to % 2

    barrier = pltpu.get_barrier_semaphore()

    def say(sem, y_to, z_to, core_to):
        pl.semaphore_signal(
            sem, inc=1, device_id=(place(y_to, z_to, core_to), ib), device_id_type=MESH
        )

    for k in range(1, n_ib):
        pl.semaphore_signal(
            barrier, inc=1, device_id=(me, lax.rem(ib + k, n_ib)), device_id_type=MESH
        )

    for k in range(1, 64):
        pl.semaphore_signal(
            barrier, inc=1, device_id=((me + k) % 64, ib), device_id_type=MESH
        )

    r = iota((256, 256), 0)
    c = iota((256, 256), 1)
    msg_ref[...] = jnp.where(
        c == (r // 4 % 2) * 128 + (r % 4) * 32 + r // 8, 1.0, 0.0
    ).astype(BF16)
    lane = iota((32, 256), 1)
    sub = iota((32, 256), 0)
    lane_f = lane.astype(F32)
    row = iota((256, 256), 0)

    for load in loads[:4]:
        load.wait()
    cb = cb_ref[...]
    sg = sg_ref[...]
    counts = jnp.zeros((256, 256), jnp.int32)
    for k in range(8):
        counts = counts + jnp.where(row == cb[k : k + 1, :], sg[k : k + 1, :], 0)
    counts = counts.astype(F32).astype(BF16)
    irr = irr_ref[...]
    irr_f = irr.astype(F32)
    order_f = ord_ref[...].astype(F32)

    loads[4].wait()
    coef_f[...] = coef_ref[...].astype(F32)
    for a in range(4):
        c_ref[:, a * 128 : (a + 1) * 128] = coef_f[:, a, :].astype(BF16)
    for load in loads[5:8]:
        load.wait()

    def choose(t, half):
        owner = (sub // 8) * 16 + (4 * half + sub // 2 % 4) * 2 + sub % 2
        position = lax.rem(ib + t, n_ib)
        owned = jnp.sum(
            jnp.where(lane == 4 * owner + position, order_f, 0.0), axis=1, keepdims=True
        )
        return jnp.where(lane_f == owned, 1.0, 0.0)

    def units(ts, half, cols):
        n = len(ts)
        pick = jnp.concatenate([choose(t, half) for t in ts], axis=0)
        irr_row = jnp.sum(pick * irr_f, axis=1, keepdims=True).astype(jnp.int32)
        pick = pick.astype(BF16)
        near = lax.dot_general(
            pick, counts, (((1,), (1,)), ((), ())), preferred_element_type=F32
        )
        kind = jnp.bitwise_xor(irr_row, irr)
        weights = jnp.concatenate(
            [jnp.where(kind == q, near, 0.0).astype(BF16) for q in range(8)], axis=0
        )
        grouped = jnp.dot(weights, c_ref[...], preferred_element_type=F32).astype(BF16)
        for q in range(8):
            for u in range(n):
                for a in range(4):
                    g_ref[u * 128 + a * 32 : u * 128 + (a + 1) * 32, q * 128 : (q + 1) * 128] = (
                        grouped[q * n * 32 + u * 32 : q * n * 32 + (u + 1) * 32, a * 128 : (a + 1) * 128]
                    )
        mixed = jnp.dot(
            g_ref[: n * 128, :], b_ref[:, :cols], preferred_element_type=F32
        ).astype(BF16)
        for u in range(n):
            z_ref[0:128, u * 128 : (u + 1) * 128] = mixed[u * 128 : (u + 1) * 128, 0:128]
            z_ref[128:256, u * 128 : (u + 1) * 128] = mixed[u * 128 : (u + 1) * 128, 128:256]
        return pick, mixed

    def pack(width):
        rows = jnp.dot(msg_ref[...], z_ref[:, :width], preferred_element_type=F32)
        return rows.reshape(32, 8, width).astype(BF16)

    def chunk_a(half):
        units((1, 2, 3), half, 256)
        send_a[half * 32 : (half + 1) * 32] = pack(384)

    def chunk_b(half):
        pick, mixed = units((0,), half, 384)
        own = jnp.dot(pick, c_ref[...], preferred_element_type=F32).astype(BF16)
        for a in range(4):
            z_ref[a * 32 : (a + 1) * 32, 128:256] = own[:, a * 128 : (a + 1) * 128]
        z_ref[128:256, 128:256] = mixed[:, 256:384]
        send_b[half * 32 : (half + 1) * 32] = pack(256)

    sends = ((send_a, recv_a), (send_b, recv_b))

    def send(which, z_to):
        src, dst = sends[which]

        def one(k, carry):
            y_to, core_to = k // 2, (core + k) % 2
            to = place(y_to, z_to, core_to)

            @pl.when(to != me)
            def _():
                pltpu.make_async_remote_copy(
                    src_ref=src.at[(z_to // 4) * 32 + y_to * 8 + (z_to % 4) * 2 + core_to],
                    dst_ref=dst.at[me],
                    send_sem=str_send.at[which],
                    recv_sem=str_recv.at[which],
                    device_id=(to, ib),
                    device_id_type=MESH,
                ).start()

            return carry

        lax.fori_loop(0, 8, one, 0)

    def await_all(ref, sem):
        some = ref.at[pl.ds(0, n_str - 1)]
        pltpu.make_async_copy(some, some, sem).wait()

    chunk_a(0)
    pl.semaphore_wait(barrier, 63 + n_ib - 1)
    send(0, 0)
    send(0, 1)
    send(0, 2)
    send(0, 3)
    chunk_a(1)
    send(0, 7)
    send(0, 4)
    send(0, 6)
    send(0, 5)
    chunk_b(0)
    send(1, 0)
    send(1, 1)
    send(1, 2)
    send(1, 3)
    chunk_b(1)
    send(1, 7)
    send(1, 4)
    send(1, 6)
    send(1, 5)
    mine = (z // 4) * 32 + y * 8 + (z % 4) * 2 + core
    recv_a[me] = send_a[mine]
    recv_b[me] = send_b[mine]
    r = iota((512, 512), 0)
    c = iota((512, 512), 1)
    from_cols = jnp.where(
        r == (c // 4 % 2) * 256 + (c // 8) * 4 + c % 4, 1.0, 0.0
    ).astype(BF16)
    for load in loads[8:]:
        load.wait()
    alpha = jnp.dot(a_ref[...], from_cols, preferred_element_type=F32).astype(BF16)
    eye = jnp.where(iota((256, 256), 0) == iota((256, 256), 1), 1.0, 0.0).astype(BF16)
    same = jnp.concatenate([as_ref[...], eye], axis=1)
    same = jnp.dot(same, from_cols, preferred_element_type=F32).astype(BF16)

    def received(ref):
        x = ref[...].astype(F32)
        return x.reshape(512, x.shape[2]).astype(BF16)

    await_all(recv_a, str_recv.at[0])
    partial = jnp.dot(alpha, received(recv_a), preferred_element_type=F32).astype(BF16)
    for u in range(3):
        part_s[u] = partial[:, u * 128 : (u + 1) * 128]

    def to_ib(u, ib_to):
        return pltpu.make_async_remote_copy(
            src_ref=part_s.at[u],
            dst_ref=part_r.at[u],
            send_sem=ib_send.at[u],
            recv_sem=ib_recv.at[u],
            device_id=(me, ib_to),
            device_id_type=MESH,
        )

    for ib_to in range(n_ib):

        @pl.when(ib_to != ib)
        def _():
            to_ib(lax.rem(ib_to - ib + n_ib - 1, n_ib), ib_to).start()

    copies = [to_ib(u, lax.rem(ib + 1 + u, n_ib)) for u in range(3)]
    await_all(recv_b, str_recv.at[1])
    x = received(recv_b)
    total = jnp.dot(alpha, x[:, 0:128], preferred_element_type=F32) + jnp.dot(
        same, x[:, 128:256], preferred_element_type=F32
    )
    for u in range(3):
        copies[u].wait_recv()
        total = total + part_r[u].astype(F32)
    out_ref[...] = total.astype(BF16)
    for u in range(3):
        copies[u].wait_send()
    await_all(send_a, str_send.at[0])
    await_all(send_b, str_send.at[1])


def local(
    n_str,
    n_ib,
    coeffs,
    block_irrep,
    couple_block,
    couple_sign,
    block_order,
    alpha_same,
    alpha_mixed,
    beta_same,
    beta_mixed,
):
    hbm = pl.BlockSpec(memory_space=pltpu.HBM)
    return pl.pallas_call(
        functools.partial(kernel, n_str, n_ib),
        out_shape=jax.ShapeDtypeStruct((256, 128), BF16),
        in_specs=[hbm] * 9,
        out_specs=pl.BlockSpec(memory_space=pltpu.VMEM),
        scratch_shapes=[
            pltpu.VMEM((256, 4, 128), BF16),
            pltpu.VMEM((256, 4, 128), F32),
            pltpu.VMEM((256, 512), BF16),
            pltpu.VMEM((1, 256), jnp.int32),
            pltpu.VMEM((8, 256), jnp.int32),
            pltpu.VMEM((8, 256), jnp.int32),
            pltpu.VMEM((1, 256), jnp.int32),
            pltpu.VMEM((1024, 384), BF16),
            pltpu.VMEM((256, 512), BF16),
            pltpu.VMEM((256, 256), BF16),
            pltpu.VMEM((256, 256), BF16),
            pltpu.VMEM((384, 1024), BF16),
            pltpu.VMEM((256, 384), BF16),
            pltpu.VMEM((64, 8, 384), BF16),
            pltpu.VMEM((64, 8, 256), BF16),
            pltpu.VMEM((64, 8, 384), BF16),
            pltpu.VMEM((64, 8, 256), BF16),
            pltpu.VMEM((3, 256, 128), BF16),
            pltpu.VMEM((3, 256, 128), BF16),
            pltpu.SemaphoreType.DMA((11,)),
            pltpu.SemaphoreType.DMA((2,)),
            pltpu.SemaphoreType.DMA((2,)),
            pltpu.SemaphoreType.DMA((3,)),
            pltpu.SemaphoreType.DMA((3,)),
            pltpu.SemaphoreType.REGULAR,
            pltpu.SemaphoreType.REGULAR,
            pltpu.SemaphoreType.REGULAR,
        ],
        compiler_params=pltpu.CompilerParams(
            collective_id=0, has_side_effects=True, vmem_limit_bytes=62 * 1024 * 1024
        ),
    )(
        coeffs.reshape(4, 256, 128).transpose(1, 0, 2),
        block_irrep.reshape(1, 256),
        couple_block.T,
        couple_sign.T,
        block_order.reshape(1, 256),
        alpha_same,
        alpha_mixed,
        beta_same.reshape(1024, 128),
        beta_mixed.reshape(2, 1024, 128),
    )


def solution(mesh):
    in_specs = (
        P("str", None),
        P(),
        P(),
        P(),
        P(),
        P(),
        P("ib", None, None),
        P(),
        P("ib", None, None, None),
    )
    body = functools.partial(local, mesh.shape["str"], mesh.shape["ib"])
    return jax.shard_map(
        body, mesh=mesh, in_specs=in_specs, out_specs=P(None, ("str", "ib")), check_vma=False
    )
```

```python
import functools

import jax
import jax.numpy as jnp
from jax import lax
from jax.experimental import pallas as pl
from jax.experimental.pallas import tpu as pltpu
from jax.sharding import PartitionSpec as P

MESH = pl.DeviceIdType.MESH
F32 = jnp.float32
BF16 = jnp.bfloat16


def iota(shape, dim):
    return lax.broadcasted_iota(jnp.int32, shape, dim)


def kernel(
    n_str,
    n_ib,
    coef_hbm,
    irr_hbm,
    cb_hbm,
    sg_hbm,
    ord_hbm,
    as_hbm,
    am_hbm,
    bs_hbm,
    bm_hbm,
    out_ref,
    coef_ref,
    coef_f,
    c_ref,
    irr_ref,
    cb_ref,
    sg_ref,
    ord_ref,
    b_ref,
    a_ref,
    as_ref,
    msg_ref,
    g_ref,
    z_ref,
    send_a,
    send_b,
    recv_a,
    recv_b,
    part_s,
    part_r,
    load_sem,
    str_send,
    str_recv,
    ib_send,
    ib_recv,
    late_sem,
    plane_sem,
    all_sem,
):
    me = lax.axis_index("str")
    ib = lax.axis_index("ib")

    loads = [
        pltpu.make_async_copy(cb_hbm, cb_ref, load_sem.at[0]),
        pltpu.make_async_copy(sg_hbm, sg_ref, load_sem.at[1]),
        pltpu.make_async_copy(irr_hbm, irr_ref, load_sem.at[2]),
        pltpu.make_async_copy(ord_hbm, ord_ref, load_sem.at[3]),
        pltpu.make_async_copy(coef_hbm, coef_ref, load_sem.at[4]),
        pltpu.make_async_copy(bm_hbm.at[0], b_ref.at[:, pl.ds(0, 128)], load_sem.at[5]),
        pltpu.make_async_copy(bm_hbm.at[1], b_ref.at[:, pl.ds(128, 128)], load_sem.at[6]),
        pltpu.make_async_copy(bs_hbm, b_ref.at[:, pl.ds(256, 128)], load_sem.at[7]),
        pltpu.make_async_copy(am_hbm.at[0], a_ref.at[:, pl.ds(0, 256)], load_sem.at[8]),
        pltpu.make_async_copy(am_hbm.at[1], a_ref.at[:, pl.ds(256, 256)], load_sem.at[9]),
        pltpu.make_async_copy(as_hbm, as_ref, load_sem.at[10]),
    ]
    for load in loads:
        load.start()

    y, z, core = me // 16, (me // 2) % 8, me % 2
    late = z >= 4

    def place(y_to, z_to, core_to):
        return (((y_to % 4) * 8) + (z_to % 8)) * 2 + core_to % 2

    barrier = pltpu.get_barrier_semaphore()

    def say(sem, y_to, z_to, core_to):
        pl.semaphore_signal(
            sem, inc=1, device_id=(place(y_to, z_to, core_to), ib), device_id_type=MESH
        )

    for k in range(1, n_ib):
        pl.semaphore_signal(
            barrier, inc=1, device_id=(me, lax.rem(ib + k, n_ib)), device_id_type=MESH
        )

    for k in range(1, 64):
        pl.semaphore_signal(
            barrier, inc=1, device_id=((me + k) % 64, ib), device_id_type=MESH
        )

    r = iota((256, 256), 0)
    c = iota((256, 256), 1)
    msg_ref[...] = jnp.where(
        c == (r // 4 % 2) * 128 + (r % 4) * 32 + r // 8, 1.0, 0.0
    ).astype(BF16)
    lane = iota((32, 256), 1)
    sub = iota((32, 256), 0)
    lane_f = lane.astype(F32)
    row = iota((256, 256), 0)

    for load in loads[:4]:
        load.wait()
    cb = cb_ref[...]
    sg = sg_ref[...]
    counts = jnp.zeros((256, 256), jnp.int32)
    for k in range(8):
        counts = counts + jnp.where(row == cb[k : k + 1, :], sg[k : k + 1, :], 0)
    counts = counts.astype(F32).astype(BF16)
    irr = irr_ref[...]
    irr_f = irr.astype(F32)
    order_f = ord_ref[...].astype(F32)

    loads[4].wait()
    coef_f[...] = coef_ref[...].astype(F32)
    for a in range(4):
        c_ref[:, a * 128 : (a + 1) * 128] = coef_f[:, a, :].astype(BF16)
    for load in loads[5:8]:
        load.wait()

    def choose(t, half):
        owner = (sub // 8) * 16 + (4 * half + sub // 2 % 4) * 2 + sub % 2
        position = lax.rem(ib + t, n_ib)
        owned = jnp.sum(
            jnp.where(lane == 4 * owner + position, order_f, 0.0), axis=1, keepdims=True
        )
        return jnp.where(lane_f == owned, 1.0, 0.0)

    def units(ts, half, cols):
        n = len(ts)
        pick = jnp.concatenate([choose(t, half) for t in ts], axis=0)
        irr_row = jnp.sum(pick * irr_f, axis=1, keepdims=True).astype(jnp.int32)
        pick = pick.astype(BF16)
        near = lax.dot_general(
            pick, counts, (((1,), (1,)), ((), ())), preferred_element_type=F32
        )
        kind = jnp.bitwise_xor(irr_row, irr)
        weights = jnp.concatenate(
            [jnp.where(kind == q, near, 0.0).astype(BF16) for q in range(8)], axis=0
        )
        grouped = jnp.dot(weights, c_ref[...], preferred_element_type=F32).astype(BF16)
        for q in range(8):
            for u in range(n):
                for a in range(4):
                    g_ref[u * 128 + a * 32 : u * 128 + (a + 1) * 32, q * 128 : (q + 1) * 128] = (
                        grouped[q * n * 32 + u * 32 : q * n * 32 + (u + 1) * 32, a * 128 : (a + 1) * 128]
                    )
        mixed = jnp.dot(
            g_ref[: n * 128, :], b_ref[:, :cols], preferred_element_type=F32
        ).astype(BF16)
        for u in range(n):
            z_ref[0:128, u * 128 : (u + 1) * 128] = mixed[u * 128 : (u + 1) * 128, 0:128]
            z_ref[128:256, u * 128 : (u + 1) * 128] = mixed[u * 128 : (u + 1) * 128, 128:256]
        return pick, mixed

    def pack(width):
        rows = jnp.dot(msg_ref[...], z_ref[:, :width], preferred_element_type=F32)
        return rows.reshape(32, 8, width).astype(BF16)

    def chunk_a(half):
        units((1, 2, 3), half, 256)
        send_a[half * 32 : (half + 1) * 32] = pack(384)

    def chunk_b(half):
        pick, mixed = units((0,), half, 384)
        own = jnp.dot(pick, c_ref[...], preferred_element_type=F32).astype(BF16)
        for a in range(4):
            z_ref[a * 32 : (a + 1) * 32, 128:256] = own[:, a * 128 : (a + 1) * 128]
        z_ref[128:256, 128:256] = mixed[:, 256:384]
        send_b[half * 32 : (half + 1) * 32] = pack(256)

    sends = ((send_a, recv_a), (send_b, recv_b))

    def send(which, z_to):
        src, dst = sends[which]

        def one(k, carry):
            y_to, core_to = k // 2, (core + k) % 2
            to = place(y_to, z_to, core_to)

            @pl.when(to != me)
            def _():
                pltpu.make_async_remote_copy(
                    src_ref=src.at[(z_to // 4) * 32 + y_to * 8 + (z_to % 4) * 2 + core_to],
                    dst_ref=dst.at[me],
                    send_sem=str_send.at[which],
                    recv_sem=str_recv.at[which],
                    device_id=(to, ib),
                    device_id_type=MESH,
                ).start()

            return carry

        lax.fori_loop(0, 8, one, 0)

    def await_all(ref, sem):
        some = ref.at[pl.ds(0, n_str - 1)]
        pltpu.make_async_copy(some, some, sem).wait()

    chunk_a(0)
    pl.semaphore_wait(barrier, 63 + n_ib - 1)
    send(0, 0)
    send(0, 1)
    send(0, 2)
    send(0, 3)
    chunk_a(1)
    send(0, 7)
    send(0, 4)
    send(0, 6)
    send(0, 5)
    chunk_b(0)
    send(1, 0)
    send(1, 1)
    send(1, 2)
    send(1, 3)
    chunk_b(1)
    send(1, 7)
    send(1, 4)
    send(1, 6)
    send(1, 5)
    mine = (z // 4) * 32 + y * 8 + (z % 4) * 2 + core
    recv_a[me] = send_a[mine]
    recv_b[me] = send_b[mine]
    r = iota((512, 512), 0)
    c = iota((512, 512), 1)
    from_cols = jnp.where(
        r == (c // 4 % 2) * 256 + (c // 8) * 4 + c % 4, 1.0, 0.0
    ).astype(BF16)
    for load in loads[8:]:
        load.wait()
    alpha = jnp.dot(a_ref[...], from_cols, preferred_element_type=F32).astype(BF16)
    eye = jnp.where(iota((256, 256), 0) == iota((256, 256), 1), 1.0, 0.0).astype(BF16)
    same = jnp.concatenate([as_ref[...], eye], axis=1)
    same = jnp.dot(same, from_cols, preferred_element_type=F32).astype(BF16)

    def received(ref):
        x = ref[...].astype(F32)
        return x.reshape(512, x.shape[2]).astype(BF16)

    await_all(recv_a, str_recv.at[0])
    partial = jnp.dot(alpha, received(recv_a), preferred_element_type=F32).astype(BF16)
    for u in range(3):
        part_s[u] = partial[:, u * 128 : (u + 1) * 128]

    def to_ib(u, ib_to):
        return pltpu.make_async_remote_copy(
            src_ref=part_s.at[u],
            dst_ref=part_r.at[u],
            send_sem=ib_send.at[u],
            recv_sem=ib_recv.at[u],
            device_id=(me, ib_to),
            device_id_type=MESH,
        )

    for ib_to in range(n_ib):

        @pl.when(ib_to != ib)
        def _():
            to_ib(lax.rem(ib_to - ib + n_ib - 1, n_ib), ib_to).start()

    copies = [to_ib(u, lax.rem(ib + 1 + u, n_ib)) for u in range(3)]
    await_all(recv_b, str_recv.at[1])
    x = received(recv_b)
    total = jnp.dot(alpha, x[:, 0:128], preferred_element_type=F32) + jnp.dot(
        same, x[:, 128:256], preferred_element_type=F32
    )
    for u in range(3):
        copies[u].wait_recv()
        total = total + part_r[u].astype(F32)
    out_ref[...] = total.astype(BF16)
    for u in range(3):
        copies[u].wait_send()
    await_all(send_a, str_send.at[0])
    await_all(send_b, str_send.at[1])


def local(
    n_str,
    n_ib,
    coeffs,
    block_irrep,
    couple_block,
    couple_sign,
    block_order,
    alpha_same,
    alpha_mixed,
    beta_same,
    beta_mixed,
):
    hbm = pl.BlockSpec(memory_space=pltpu.HBM)
    return pl.pallas_call(
        functools.partial(kernel, n_str, n_ib),
        out_shape=pltpu.VMEM((256, 128), BF16),
        in_specs=[hbm] * 9,
        out_specs=pl.BlockSpec(memory_space=pltpu.VMEM),
        scratch_shapes=[
            pltpu.VMEM((256, 4, 128), BF16),
            pltpu.VMEM((256, 4, 128), F32),
            pltpu.VMEM((256, 512), BF16),
            pltpu.VMEM((1, 256), jnp.int32),
            pltpu.VMEM((8, 256), jnp.int32),
            pltpu.VMEM((8, 256), jnp.int32),
            pltpu.VMEM((1, 256), jnp.int32),
            pltpu.VMEM((1024, 384), BF16),
            pltpu.VMEM((256, 512), BF16),
            pltpu.VMEM((256, 256), BF16),
            pltpu.VMEM((256, 256), BF16),
            pltpu.VMEM((384, 1024), BF16),
            pltpu.VMEM((256, 384), BF16),
            pltpu.VMEM((64, 8, 384), BF16),
            pltpu.VMEM((64, 8, 256), BF16),
            pltpu.VMEM((64, 8, 384), BF16),
            pltpu.VMEM((64, 8, 256), BF16),
            pltpu.VMEM((3, 256, 128), BF16),
            pltpu.VMEM((3, 256, 128), BF16),
            pltpu.SemaphoreType.DMA((11,)),
            pltpu.SemaphoreType.DMA((2,)),
            pltpu.SemaphoreType.DMA((2,)),
            pltpu.SemaphoreType.DMA((3,)),
            pltpu.SemaphoreType.DMA((3,)),
            pltpu.SemaphoreType.REGULAR,
            pltpu.SemaphoreType.REGULAR,
            pltpu.SemaphoreType.REGULAR,
        ],
        compiler_params=pltpu.CompilerParams(
            collective_id=0, has_side_effects=True, vmem_limit_bytes=62 * 1024 * 1024
        ),
    )(
        coeffs.reshape(4, 256, 128).transpose(1, 0, 2),
        block_irrep.reshape(1, 256),
        couple_block.T,
        couple_sign.T,
        block_order.reshape(1, 256),
        alpha_same,
        alpha_mixed,
        beta_same.reshape(1024, 128),
        beta_mixed.reshape(2, 1024, 128),
    )


def solution(mesh):
    in_specs = (
        P("str", None),
        P(),
        P(),
        P(),
        P(),
        P(),
        P("ib", None, None),
        P(),
        P("ib", None, None, None),
    )
    body = functools.partial(local, mesh.shape["str"], mesh.shape["ib"])
    return jax.shard_map(
        body, mesh=mesh, in_specs=in_specs, out_specs=P(None, ("str", "ib")), check_vma=False
    )
```

```python
import functools

import jax
import jax.numpy as jnp
from jax import lax
from jax.experimental import pallas as pl
from jax.experimental.pallas import tpu as pltpu
from jax.sharding import PartitionSpec as P

MESH = pl.DeviceIdType.MESH
F32 = jnp.float32
BF16 = jnp.bfloat16
NEAR = (0, 1, 2, 3)
FAR = (7, 4, 6, 5)


def iota(shape, dim):
    return lax.broadcasted_iota(jnp.int32, shape, dim)


def kernel(
    n_str,
    n_ib,
    coef_hbm,
    irr_hbm,
    cb_hbm,
    sg_hbm,
    ord_hbm,
    as_hbm,
    am_hbm,
    bs_hbm,
    bm_hbm,
    out_ref,
    coef_ref,
    coef_f,
    c_ref,
    irr_ref,
    cb_ref,
    sg_ref,
    ord_ref,
    b_ref,
    a_ref,
    as_ref,
    msg_ref,
    alpha_ref,
    same_ref,
    g_ref,
    z_ref,
    send_a,
    send_c,
    send_b,
    recv_a,
    recv_c,
    recv_b,
    part_s,
    part_r,
    load_sem,
    str_send,
    str_recv,
    ib_send,
    ib_recv,
    late_sem,
    plane_sem,
    all_sem,
):
    me = lax.axis_index("str")
    ib = lax.axis_index("ib")

    loads = [
        pltpu.make_async_copy(cb_hbm, cb_ref, load_sem.at[0]),
        pltpu.make_async_copy(sg_hbm, sg_ref, load_sem.at[1]),
        pltpu.make_async_copy(irr_hbm, irr_ref, load_sem.at[2]),
        pltpu.make_async_copy(ord_hbm, ord_ref, load_sem.at[3]),
        pltpu.make_async_copy(coef_hbm, coef_ref, load_sem.at[4]),
        pltpu.make_async_copy(bm_hbm.at[0], b_ref.at[:, pl.ds(0, 128)], load_sem.at[5]),
        pltpu.make_async_copy(bm_hbm.at[1], b_ref.at[:, pl.ds(128, 128)], load_sem.at[6]),
        pltpu.make_async_copy(bs_hbm, b_ref.at[:, pl.ds(256, 128)], load_sem.at[7]),
        pltpu.make_async_copy(am_hbm.at[0], a_ref.at[:, pl.ds(0, 256)], load_sem.at[8]),
        pltpu.make_async_copy(am_hbm.at[1], a_ref.at[:, pl.ds(256, 256)], load_sem.at[9]),
        pltpu.make_async_copy(as_hbm, as_ref, load_sem.at[10]),
    ]
    for load in loads:
        load.start()

    y, z, core = me // 16, (me // 2) % 8, me % 2
    late = z >= 4

    def place(y_to, z_to, core_to):
        return (((y_to % 4) * 8) + (z_to % 8)) * 2 + core_to % 2

    barrier = pltpu.get_barrier_semaphore()

    def say(sem, y_to, z_to, core_to):
        pl.semaphore_signal(
            sem, inc=1, device_id=(place(y_to, z_to, core_to), ib), device_id_type=MESH
        )

    for k in range(1, n_ib):
        pl.semaphore_signal(
            barrier, inc=1, device_id=(me, lax.rem(ib + k, n_ib)), device_id_type=MESH
        )

    for k in range(1, 64):
        pl.semaphore_signal(
            barrier, inc=1, device_id=((me + k) % 64, ib), device_id_type=MESH
        )

    r = iota((256, 256), 0)
    c = iota((256, 256), 1)
    msg_ref[...] = jnp.where(
        c == (r // 4 % 2) * 128 + (r % 4) * 32 + r // 8, 1.0, 0.0
    ).astype(BF16)
    lane = iota((32, 256), 1)
    sub = iota((32, 256), 0)
    lane_f = lane.astype(F32)
    row = iota((256, 256), 0)

    for load in loads[:4]:
        load.wait()
    cb = cb_ref[...]
    sg = sg_ref[...]
    counts = jnp.zeros((256, 256), jnp.int32)
    for k in range(8):
        counts = counts + jnp.where(row == cb[k : k + 1, :], sg[k : k + 1, :], 0)
    counts = counts.astype(F32).astype(BF16)
    irr = irr_ref[...]
    irr_f = irr.astype(F32)
    order_f = ord_ref[...].astype(F32)

    loads[4].wait()
    coef_f[...] = coef_ref[...].astype(F32)
    for a in range(4):
        c_ref[:, a * 128 : (a + 1) * 128] = coef_f[:, a, :].astype(BF16)
    for load in loads[5:8]:
        load.wait()

    peers = [jnp.where(ib > u, u, u + 1) for u in range(3)]

    def choose(position, half):
        owner = (sub // 8) * 16 + (4 * half + sub // 2 % 4) * 2 + sub % 2
        owned = jnp.sum(
            jnp.where(lane == 4 * owner + position, order_f, 0.0), axis=1, keepdims=True
        )
        return jnp.where(lane_f == owned, 1.0, 0.0)

    def units(positions, half, cols):
        n = len(positions)
        pick = jnp.concatenate([choose(at, half) for at in positions], axis=0)
        irr_row = jnp.sum(pick * irr_f, axis=1, keepdims=True).astype(jnp.int32)
        pick = pick.astype(BF16)
        near = lax.dot_general(
            pick, counts, (((1,), (1,)), ((), ())), preferred_element_type=F32
        )
        kind = jnp.bitwise_xor(irr_row, irr)
        weights = jnp.concatenate(
            [jnp.where(kind == q, near, 0.0).astype(BF16) for q in range(8)], axis=0
        )
        grouped = jnp.dot(weights, c_ref[...], preferred_element_type=F32).astype(BF16)
        for q in range(8):
            for u in range(n):
                for a in range(4):
                    g_ref[u * 128 + a * 32 : u * 128 + (a + 1) * 32, q * 128 : (q + 1) * 128] = (
                        grouped[q * n * 32 + u * 32 : q * n * 32 + (u + 1) * 32, a * 128 : (a + 1) * 128]
                    )
        mixed = jnp.dot(
            g_ref[: n * 128, :], b_ref[:, :cols], preferred_element_type=F32
        ).astype(BF16)
        for u in range(n):
            z_ref[0:128, u * 128 : (u + 1) * 128] = mixed[u * 128 : (u + 1) * 128, 0:128]
            z_ref[128:256, u * 128 : (u + 1) * 128] = mixed[u * 128 : (u + 1) * 128, 128:256]
        return pick, mixed

    def pack(width):
        rows = jnp.dot(msg_ref[...], z_ref[:, :width], preferred_element_type=F32)
        return rows.reshape(32, 8, width).astype(BF16)

    def chunk_a(half):
        units(peers, half, 256)
        rows = pack(384)
        send_a[half * 32 : (half + 1) * 32] = rows[:, :, :128]
        send_c[half * 32 : (half + 1) * 32] = rows[:, :, 128:]

    def chunk_b(half):
        pick, mixed = units([ib], half, 384)
        own = jnp.dot(pick, c_ref[...], preferred_element_type=F32).astype(BF16)
        for a in range(4):
            z_ref[a * 32 : (a + 1) * 32, 128:256] = own[:, a * 128 : (a + 1) * 128]
        z_ref[128:256, 128:256] = mixed[:, 256:384]
        send_b[half * 32 : (half + 1) * 32] = pack(256)

    sends = ((send_a, recv_a), (send_c, recv_c), (send_b, recv_b))

    def send(which, z_to):
        src, dst = sends[which]

        def one(k, carry):
            y_to, core_to = k // 2, (core + k) % 2
            to = place(y_to, z_to, core_to)

            @pl.when(to != me)
            def _():
                pltpu.make_async_remote_copy(
                    src_ref=src.at[(z_to // 4) * 32 + y_to * 8 + (z_to % 4) * 2 + core_to],
                    dst_ref=dst.at[me],
                    send_sem=str_send.at[which],
                    recv_sem=str_recv.at[which],
                    device_id=(to, ib),
                    device_id_type=MESH,
                ).start()

            return carry

        lax.fori_loop(0, 8, one, 0)

    def await_all(ref, sem):
        some = ref.at[pl.ds(0, n_str - 1)]
        pltpu.make_async_copy(some, some, sem).wait()

    chunk_a(0)
    pl.semaphore_wait(barrier, 63 + n_ib - 1)
    for z_to in NEAR:
        send(0, z_to)
    chunk_a(1)
    for z_to in FAR:
        send(0, z_to)
    for z_to in NEAR:
        send(1, z_to)
    chunk_b(0)
    for z_to in FAR[:2]:
        send(1, z_to)
    chunk_b(1)
    for z_to in FAR[2:]:
        send(1, z_to)
    for z_to in NEAR:
        send(2, z_to)
    for z_to in (4, 5, 6, 7):
        send(2, z_to)

    mine = (z // 4) * 32 + y * 8 + (z % 4) * 2 + core
    recv_a[me] = send_a[mine]
    recv_c[me] = send_c[mine]
    def received(ref):
        x = ref[...].astype(F32)
        return x.reshape(512, x.shape[2]).astype(BF16)

    def to_peer(u):
        slot = jnp.where(ib < peers[u], ib, ib - 1)
        return pltpu.make_async_remote_copy(
            src_ref=part_s.at[u],
            dst_ref=part_r.at[slot],
            send_sem=ib_send.at[u],
            recv_sem=ib_recv.at[slot],
            device_id=(me, peers[u]),
            device_id_type=MESH,
        )

    def first_peer():
        await_all(recv_a, str_recv.at[0])
        part_s[0] = jnp.dot(
            alpha_ref[...], received(recv_a), preferred_element_type=F32
        ).astype(BF16)
        to_peer(0).start()

    recv_b[me] = send_b[mine]
    r = iota((512, 512), 0)
    c = iota((512, 512), 1)
    from_cols = jnp.where(
        r == (c // 4 % 2) * 256 + (c // 8) * 4 + c % 4, 1.0, 0.0
    ).astype(BF16)
    for load in loads[8:]:
        load.wait()
    alpha_ref[...] = jnp.dot(a_ref[...], from_cols, preferred_element_type=F32).astype(BF16)
    eye = jnp.where(iota((256, 256), 0) == iota((256, 256), 1), 1.0, 0.0).astype(BF16)
    same = jnp.concatenate([as_ref[...], eye], axis=1)
    same_ref[...] = jnp.dot(same, from_cols, preferred_element_type=F32).astype(BF16)

    first_peer()
    await_all(recv_c, str_recv.at[1])
    partial = jnp.dot(alpha_ref[...], received(recv_c), preferred_element_type=F32).astype(BF16)
    for u in (1, 2):
        part_s[u] = partial[:, (u - 1) * 128 : u * 128]
        to_peer(u).start()
    await_all(recv_b, str_recv.at[2])
    x = received(recv_b)
    total = jnp.dot(alpha_ref[...], x[:, 0:128], preferred_element_type=F32) + jnp.dot(
        same_ref[...], x[:, 128:256], preferred_element_type=F32
    )
    for k in range(3):
        pltpu.make_async_copy(part_r.at[k], part_r.at[k], ib_recv.at[k]).wait()
        total = total + part_r[k].astype(F32)
    out_ref[...] = total.astype(BF16)
    for u in range(3):
        to_peer(u).wait_send()
    await_all(send_a, str_send.at[0])
    await_all(send_c, str_send.at[1])
    await_all(send_b, str_send.at[2])


def local(
    n_str,
    n_ib,
    coeffs,
    block_irrep,
    couple_block,
    couple_sign,
    block_order,
    alpha_same,
    alpha_mixed,
    beta_same,
    beta_mixed,
):
    hbm = pl.BlockSpec(memory_space=pltpu.HBM)
    return pl.pallas_call(
        functools.partial(kernel, n_str, n_ib),
        out_shape=pltpu.VMEM((256, 128), BF16),
        in_specs=[hbm] * 9,
        out_specs=pl.BlockSpec(memory_space=pltpu.VMEM),
        scratch_shapes=[
            pltpu.VMEM((256, 4, 128), BF16),
            pltpu.VMEM((256, 4, 128), F32),
            pltpu.VMEM((256, 512), BF16),
            pltpu.VMEM((1, 256), jnp.int32),
            pltpu.VMEM((8, 256), jnp.int32),
            pltpu.VMEM((8, 256), jnp.int32),
            pltpu.VMEM((1, 256), jnp.int32),
            pltpu.VMEM((1024, 384), BF16),
            pltpu.VMEM((256, 512), BF16),
            pltpu.VMEM((256, 256), BF16),
            pltpu.VMEM((256, 256), BF16),
            pltpu.VMEM((256, 512), BF16),
            pltpu.VMEM((256, 512), BF16),
            pltpu.VMEM((384, 1024), BF16),
            pltpu.VMEM((256, 384), BF16),
            pltpu.VMEM((64, 8, 128), BF16),
            pltpu.VMEM((64, 8, 256), BF16),
            pltpu.VMEM((64, 8, 256), BF16),
            pltpu.VMEM((64, 8, 128), BF16),
            pltpu.VMEM((64, 8, 256), BF16),
            pltpu.VMEM((64, 8, 256), BF16),
            pltpu.VMEM((3, 256, 128), BF16),
            pltpu.VMEM((3, 256, 128), BF16),
            pltpu.SemaphoreType.DMA((11,)),
            pltpu.SemaphoreType.DMA((3,)),
            pltpu.SemaphoreType.DMA((3,)),
            pltpu.SemaphoreType.DMA((3,)),
            pltpu.SemaphoreType.DMA((3,)),
            pltpu.SemaphoreType.REGULAR,
            pltpu.SemaphoreType.REGULAR,
            pltpu.SemaphoreType.REGULAR,
        ],
        compiler_params=pltpu.CompilerParams(
            collective_id=0, has_side_effects=True, vmem_limit_bytes=62 * 1024 * 1024
        ),
    )(
        coeffs.reshape(4, 256, 128).transpose(1, 0, 2),
        block_irrep.reshape(1, 256),
        couple_block.T,
        couple_sign.T,
        block_order.reshape(1, 256),
        alpha_same,
        alpha_mixed,
        beta_same.reshape(1024, 128),
        beta_mixed.reshape(2, 1024, 128),
    )


def solution(mesh):
    in_specs = (
        P("str", None),
        P(),
        P(),
        P(),
        P(),
        P(),
        P("ib", None, None),
        P(),
        P("ib", None, None, None),
    )
    body = functools.partial(local, mesh.shape["str"], mesh.shape["ib"])
    return jax.shard_map(
        body, mesh=mesh, in_specs=in_specs, out_specs=P(None, ("str", "ib")), check_vma=False
    )
```

```python
import functools

import jax
import jax.numpy as jnp
from jax import lax
from jax.experimental import pallas as pl
from jax.experimental.pallas import tpu as pltpu
from jax.sharding import PartitionSpec as P

MESH = pl.DeviceIdType.MESH
F32 = jnp.float32
BF16 = jnp.bfloat16
NEAR = (0, 1, 2, 3)
FAR = (7, 4, 6, 5)
FAR_LAST = (4, 5, 6, 7)


def iota(shape, dim):
    return lax.broadcasted_iota(jnp.int32, shape, dim)


def kernel(
    n_str,
    n_ib,
    coef_hbm,
    irr_hbm,
    cb_hbm,
    sg_hbm,
    ord_hbm,
    as_hbm,
    am_hbm,
    bs_hbm,
    bm_hbm,
    out_ref,
    coef_ref,
    coef_f,
    c_ref,
    irr_ref,
    cb_ref,
    sg_ref,
    ord_ref,
    b_ref,
    a_ref,
    as_ref,
    msg_ref,
    alpha_ref,
    same_ref,
    g_ref,
    z_ref,
    send_a,
    send_c,
    send_b,
    recv_a,
    recv_c,
    recv_b,
    part_s,
    part_r,
    load_sem,
    str_send,
    str_recv,
    ib_send,
    ib_recv,
    late_sem,
    plane_sem,
    all_sem,
):
    me = lax.axis_index("str")
    ib = lax.axis_index("ib")

    loads = [
        pltpu.make_async_copy(cb_hbm, cb_ref, load_sem.at[0]),
        pltpu.make_async_copy(sg_hbm, sg_ref, load_sem.at[1]),
        pltpu.make_async_copy(irr_hbm, irr_ref, load_sem.at[2]),
        pltpu.make_async_copy(ord_hbm, ord_ref, load_sem.at[3]),
        pltpu.make_async_copy(coef_hbm, coef_ref, load_sem.at[4]),
        pltpu.make_async_copy(bm_hbm.at[0], b_ref.at[:, pl.ds(0, 128)], load_sem.at[5]),
        pltpu.make_async_copy(bm_hbm.at[1], b_ref.at[:, pl.ds(128, 128)], load_sem.at[6]),
        pltpu.make_async_copy(bs_hbm, b_ref.at[:, pl.ds(256, 128)], load_sem.at[7]),
        pltpu.make_async_copy(am_hbm.at[0], a_ref.at[:, pl.ds(0, 256)], load_sem.at[8]),
        pltpu.make_async_copy(am_hbm.at[1], a_ref.at[:, pl.ds(256, 256)], load_sem.at[9]),
        pltpu.make_async_copy(as_hbm, as_ref, load_sem.at[10]),
    ]
    for load in loads:
        load.start()

    y, z, core = me // 16, (me // 2) % 8, me % 2

    def place(y_to, z_to, core_to):
        return (((y_to % 4) * 8) + (z_to % 8)) * 2 + core_to % 2

    barrier = pltpu.get_barrier_semaphore()

    for k in range(1, n_ib):
        pl.semaphore_signal(
            barrier, inc=1, device_id=(me, lax.rem(ib + k, n_ib)), device_id_type=MESH
        )

    for k in range(1, 64):
        pl.semaphore_signal(
            barrier, inc=1, device_id=((me + k) % 64, ib), device_id_type=MESH
        )

    r = iota((256, 256), 0)
    c = iota((256, 256), 1)
    msg_ref[...] = jnp.where(
        c == (r // 4 % 2) * 128 + (r % 4) * 32 + r // 8, 1.0, 0.0
    ).astype(BF16)
    lane = iota((32, 256), 1)
    sub = iota((32, 256), 0)
    lane_f = lane.astype(F32)
    row = iota((256, 256), 0)

    for load in loads[:4]:
        load.wait()
    cb = cb_ref[...]
    sg = sg_ref[...]
    counts = jnp.zeros((256, 256), jnp.int32)
    for k in range(8):
        counts = counts + jnp.where(row == cb[k : k + 1, :], sg[k : k + 1, :], 0)
    counts = counts.astype(F32).astype(BF16)
    irr = irr_ref[...]
    irr_f = irr.astype(F32)
    order_f = ord_ref[...].astype(F32)

    loads[4].wait()
    coef_f[...] = coef_ref[...].astype(F32)
    for a in range(4):
        c_ref[:, a * 128 : (a + 1) * 128] = coef_f[:, a, :].astype(BF16)
    for load in loads[5:8]:
        load.wait()

    peers = [jnp.where(ib > u, u, u + 1) for u in range(3)]

    def choose(position, half):
        owner = (sub // 8) * 16 + (4 * half + sub // 2 % 4) * 2 + sub % 2
        owned = jnp.sum(
            jnp.where(lane == 4 * owner + position, order_f, 0.0), axis=1, keepdims=True
        )
        return jnp.where(lane_f == owned, 1.0, 0.0)

    def units(positions, half, cols):
        n = len(positions)
        pick = jnp.concatenate([choose(at, half) for at in positions], axis=0)
        irr_row = jnp.sum(pick * irr_f, axis=1, keepdims=True).astype(jnp.int32)
        pick = pick.astype(BF16)
        near = lax.dot_general(
            pick, counts, (((1,), (1,)), ((), ())), preferred_element_type=F32
        )
        kind = jnp.bitwise_xor(irr_row, irr)
        weights = jnp.concatenate(
            [jnp.where(kind == q, near, 0.0).astype(BF16) for q in range(8)], axis=0
        )
        grouped = jnp.dot(weights, c_ref[...], preferred_element_type=F32).astype(BF16)
        for q in range(8):
            for u in range(n):
                for a in range(4):
                    g_ref[u * 128 + a * 32 : u * 128 + (a + 1) * 32, q * 128 : (q + 1) * 128] = (
                        grouped[q * n * 32 + u * 32 : q * n * 32 + (u + 1) * 32, a * 128 : (a + 1) * 128]
                    )
        mixed = jnp.dot(
            g_ref[: n * 128, :], b_ref[:, :cols], preferred_element_type=F32
        ).astype(BF16)
        for u in range(n):
            z_ref[0:128, u * 128 : (u + 1) * 128] = mixed[u * 128 : (u + 1) * 128, 0:128]
            z_ref[128:256, u * 128 : (u + 1) * 128] = mixed[u * 128 : (u + 1) * 128, 128:256]
        return pick, mixed

    def pack(width):
        rows = jnp.dot(msg_ref[...], z_ref[:, :width], preferred_element_type=F32)
        return rows.reshape(32, 8, width).astype(BF16)

    def chunk_a(half):
        units(peers, half, 256)
        rows = pack(384)
        send_a[half * 32 : (half + 1) * 32] = rows[:, :, :128]
        send_c[half * 32 : (half + 1) * 32] = rows[:, :, 128:]

    def chunk_b(half):
        pick, mixed = units([ib], half, 384)
        own = jnp.dot(pick, c_ref[...], preferred_element_type=F32).astype(BF16)
        for a in range(4):
            z_ref[a * 32 : (a + 1) * 32, 128:256] = own[:, a * 128 : (a + 1) * 128]
        z_ref[128:256, 128:256] = mixed[:, 256:384]
        send_b[half * 32 : (half + 1) * 32] = pack(256)

    sends = ((send_a, recv_a), (send_c, recv_c), (send_b, recv_b))

    def send(which, z_to):
        src, dst = sends[which]

        def one(k, carry):
            y_to, core_to = k // 2, (core + k) % 2
            to = place(y_to, z_to, core_to)

            @pl.when(to != me)
            def _():
                pltpu.make_async_remote_copy(
                    src_ref=src.at[(z_to // 4) * 32 + y_to * 8 + (z_to % 4) * 2 + core_to],
                    dst_ref=dst.at[me],
                    send_sem=str_send.at[which],
                    recv_sem=str_recv.at[which],
                    device_id=(to, ib),
                    device_id_type=MESH,
                ).start()

            return carry

        lax.fori_loop(0, 8, one, 0)

    def await_all(ref, sem):
        some = ref.at[pl.ds(0, n_str - 1)]
        pltpu.make_async_copy(some, some, sem).wait()

    chunk_a(0)
    pl.semaphore_wait(barrier, 63 + n_ib - 1)
    for z_to in NEAR:
        send(0, z_to)
    chunk_a(1)
    for z_to in FAR:
        send(0, z_to)
    for z_to in NEAR:
        send(1, z_to)
    chunk_b(0)
    for z_to in FAR[:2]:
        send(1, z_to)
    chunk_b(1)
    for z_to in FAR[2:]:
        send(1, z_to)
    for z_to in NEAR:
        send(2, z_to)
    for z_to in FAR_LAST:
        send(2, z_to)

    mine = (z // 4) * 32 + y * 8 + (z % 4) * 2 + core
    recv_a[me] = send_a[mine]
    recv_c[me] = send_c[mine]
    def received(ref):
        x = ref[...].astype(F32)
        return x.reshape(512, x.shape[2]).astype(BF16)

    def to_peer(u):
        slot = jnp.where(ib < peers[u], ib, ib - 1)
        return pltpu.make_async_remote_copy(
            src_ref=part_s.at[u],
            dst_ref=part_r.at[slot],
            send_sem=ib_send.at[u],
            recv_sem=ib_recv.at[slot],
            device_id=(me, peers[u]),
            device_id_type=MESH,
        )

    def first_peer():
        await_all(recv_a, str_recv.at[0])
        part_s[0] = jnp.dot(
            alpha_ref[...], received(recv_a), preferred_element_type=F32
        ).astype(BF16)
        to_peer(0).start()

    recv_b[me] = send_b[mine]
    r = iota((512, 512), 0)
    c = iota((512, 512), 1)
    from_cols = jnp.where(
        r == (c // 4 % 2) * 256 + (c // 8) * 4 + c % 4, 1.0, 0.0
    ).astype(BF16)
    for load in loads[8:]:
        load.wait()
    alpha_ref[...] = jnp.dot(a_ref[...], from_cols, preferred_element_type=F32).astype(BF16)
    eye = jnp.where(iota((256, 256), 0) == iota((256, 256), 1), 1.0, 0.0).astype(BF16)
    same = jnp.concatenate([as_ref[...], eye], axis=1)
    same_ref[...] = jnp.dot(same, from_cols, preferred_element_type=F32).astype(BF16)

    first_peer()
    await_all(recv_c, str_recv.at[1])
    partial = jnp.dot(alpha_ref[...], received(recv_c), preferred_element_type=F32).astype(BF16)
    for u in (1, 2):
        part_s[u] = partial[:, (u - 1) * 128 : u * 128]
        to_peer(u).start()
    await_all(recv_b, str_recv.at[2])
    x = received(recv_b)
    total = jnp.dot(alpha_ref[...], x[:, 0:128], preferred_element_type=F32) + jnp.dot(
        same_ref[...], x[:, 128:256], preferred_element_type=F32
    )
    for k in range(3):
        pltpu.make_async_copy(part_r.at[k], part_r.at[k], ib_recv.at[k]).wait()
        total = total + part_r[k].astype(F32)
    out_ref[...] = total.astype(BF16)
    for u in range(3):
        to_peer(u).wait_send()
    await_all(send_a, str_send.at[0])
    await_all(send_c, str_send.at[1])
    await_all(send_b, str_send.at[2])


def local(
    n_str,
    n_ib,
    coeffs,
    block_irrep,
    couple_block,
    couple_sign,
    block_order,
    alpha_same,
    alpha_mixed,
    beta_same,
    beta_mixed,
):
    hbm = pl.BlockSpec(memory_space=pltpu.HBM)
    return pl.pallas_call(
        functools.partial(kernel, n_str, n_ib),
        out_shape=pltpu.VMEM((256, 128), BF16),
        in_specs=[hbm] * 9,
        out_specs=pl.BlockSpec(memory_space=pltpu.VMEM),
        scratch_shapes=[
            pltpu.VMEM((256, 4, 128), BF16),
            pltpu.VMEM((256, 4, 128), F32),
            pltpu.VMEM((256, 512), BF16),
            pltpu.VMEM((1, 256), jnp.int32),
            pltpu.VMEM((8, 256), jnp.int32),
            pltpu.VMEM((8, 256), jnp.int32),
            pltpu.VMEM((1, 256), jnp.int32),
            pltpu.VMEM((1024, 384), BF16),
            pltpu.VMEM((256, 512), BF16),
            pltpu.VMEM((256, 256), BF16),
            pltpu.VMEM((256, 256), BF16),
            pltpu.VMEM((256, 512), BF16),
            pltpu.VMEM((256, 512), BF16),
            pltpu.VMEM((384, 1024), BF16),
            pltpu.VMEM((256, 384), BF16),
            pltpu.VMEM((64, 8, 128), BF16),
            pltpu.VMEM((64, 8, 256), BF16),
            pltpu.VMEM((64, 8, 256), BF16),
            pltpu.VMEM((64, 8, 128), BF16),
            pltpu.VMEM((64, 8, 256), BF16),
            pltpu.VMEM((64, 8, 256), BF16),
            pltpu.VMEM((3, 256, 128), BF16),
            pltpu.VMEM((3, 256, 128), BF16),
            pltpu.SemaphoreType.DMA((11,)),
            pltpu.SemaphoreType.DMA((3,)),
            pltpu.SemaphoreType.DMA((3,)),
            pltpu.SemaphoreType.DMA((3,)),
            pltpu.SemaphoreType.DMA((3,)),
            pltpu.SemaphoreType.REGULAR,
            pltpu.SemaphoreType.REGULAR,
            pltpu.SemaphoreType.REGULAR,
        ],
        compiler_params=pltpu.CompilerParams(
            collective_id=0, has_side_effects=True, vmem_limit_bytes=62 * 1024 * 1024
        ),
    )(
        coeffs.reshape(4, 256, 128).transpose(1, 0, 2),
        block_irrep.reshape(1, 256),
        couple_block.T,
        couple_sign.T,
        block_order.reshape(1, 256),
        alpha_same,
        alpha_mixed,
        beta_same.reshape(1024, 128),
        beta_mixed.reshape(2, 1024, 128),
    )


def solution(mesh):
    in_specs = (
        P("str", None),
        P(),
        P(),
        P(),
        P(),
        P(),
        P("ib", None, None),
        P(),
        P("ib", None, None, None),
    )
    body = functools.partial(local, mesh.shape["str"], mesh.shape["ib"])
    return jax.shard_map(
        body, mesh=mesh, in_specs=in_specs, out_specs=P(None, ("str", "ib")), check_vma=False
    )
```

```python
import functools

import jax
import jax.numpy as jnp
from jax import lax
from jax.experimental import pallas as pl
from jax.experimental.pallas import tpu as pltpu
from jax.sharding import PartitionSpec as P

MESH = pl.DeviceIdType.MESH
F32 = jnp.float32
BF16 = jnp.bfloat16
NEAR = (0, 1, 2, 3)
FAR = (4, 7, 5, 6)
NEAR_LAST = ((0, 0), (0, 1), (1, 0), (0, 2), (1, 1), (0, 3), (2, 0), (1, 2), (2, 1), (1, 3), (3, 0), (2, 2), (3, 1), (2, 3), (3, 2), (3, 3))
FAR_LAST = ((4, 0), (5, 0), (6, 0), (7, 0), (4, 1), (4, 2), (4, 3), (5, 1), (5, 2), (5, 3), (6, 1), (6, 2), (6, 3), (7, 1), (7, 2), (7, 3))


def iota(shape, dim):
    return lax.broadcasted_iota(jnp.int32, shape, dim)


def kernel(
    n_str,
    n_ib,
    coef_hbm,
    irr_hbm,
    cb_hbm,
    sg_hbm,
    ord_hbm,
    as_hbm,
    am_hbm,
    bs_hbm,
    bm_hbm,
    out_ref,
    coef_ref,
    coef_f,
    c_ref,
    irr_ref,
    cb_ref,
    sg_ref,
    ord_ref,
    b_ref,
    a_ref,
    as_ref,
    msg_ref,
    alpha_ref,
    same_ref,
    g_ref,
    z_ref,
    send_a,
    send_c,
    send_b,
    recv_a,
    recv_c,
    recv_b,
    part_s,
    part_r,
    load_sem,
    str_send,
    str_recv,
    ib_send,
    ib_recv,
    late_sem,
    plane_sem,
    all_sem,
):
    me = lax.axis_index("str")
    ib = lax.axis_index("ib")

    loads = [
        pltpu.make_async_copy(cb_hbm, cb_ref, load_sem.at[0]),
        pltpu.make_async_copy(sg_hbm, sg_ref, load_sem.at[1]),
        pltpu.make_async_copy(irr_hbm, irr_ref, load_sem.at[2]),
        pltpu.make_async_copy(ord_hbm, ord_ref, load_sem.at[3]),
        pltpu.make_async_copy(coef_hbm, coef_ref, load_sem.at[4]),
        pltpu.make_async_copy(bm_hbm.at[0], b_ref.at[:, pl.ds(0, 128)], load_sem.at[5]),
        pltpu.make_async_copy(bm_hbm.at[1], b_ref.at[:, pl.ds(128, 128)], load_sem.at[6]),
        pltpu.make_async_copy(bs_hbm, b_ref.at[:, pl.ds(256, 128)], load_sem.at[7]),
        pltpu.make_async_copy(am_hbm.at[0], a_ref.at[:, pl.ds(0, 256)], load_sem.at[8]),
        pltpu.make_async_copy(am_hbm.at[1], a_ref.at[:, pl.ds(256, 256)], load_sem.at[9]),
        pltpu.make_async_copy(as_hbm, as_ref, load_sem.at[10]),
    ]
    for load in loads:
        load.start()

    y, z, core = me // 16, (me // 2) % 8, me % 2

    def place(y_to, z_to, core_to):
        return (((y_to % 4) * 8) + (z_to % 8)) * 2 + core_to % 2

    barrier = pltpu.get_barrier_semaphore()

    for k in range(1, n_ib):
        pl.semaphore_signal(
            barrier, inc=1, device_id=(me, lax.rem(ib + k, n_ib)), device_id_type=MESH
        )

    for k in range(1, 64):
        pl.semaphore_signal(
            barrier, inc=1, device_id=((me + k) % 64, ib), device_id_type=MESH
        )

    r = iota((256, 256), 0)
    c = iota((256, 256), 1)
    msg_ref[...] = jnp.where(
        c == (r // 4 % 2) * 128 + (r % 4) * 32 + r // 8, 1.0, 0.0
    ).astype(BF16)
    lane = iota((32, 256), 1)
    sub = iota((32, 256), 0)
    lane_f = lane.astype(F32)
    row = iota((256, 256), 0)

    for load in loads[:4]:
        load.wait()
    cb = cb_ref[...]
    sg = sg_ref[...]
    counts = jnp.zeros((256, 256), jnp.int32)
    for k in range(8):
        counts = counts + jnp.where(row == cb[k : k + 1, :], sg[k : k + 1, :], 0)
    counts = counts.astype(F32).astype(BF16)
    irr = irr_ref[...]
    irr_f = irr.astype(F32)
    order_f = ord_ref[...].astype(F32)

    loads[4].wait()
    coef_f[...] = coef_ref[...].astype(F32)
    for a in range(4):
        c_ref[:, a * 128 : (a + 1) * 128] = coef_f[:, a, :].astype(BF16)
    for load in loads[5:8]:
        load.wait()

    peers = [jnp.where(ib > u, u, u + 1) for u in range(3)]

    def choose(position, half):
        owner = (sub // 8) * 16 + (4 * half + sub // 2 % 4) * 2 + sub % 2
        owned = jnp.sum(
            jnp.where(lane == 4 * owner + position, order_f, 0.0), axis=1, keepdims=True
        )
        return jnp.where(lane_f == owned, 1.0, 0.0)

    def units(positions, half, cols):
        n = len(positions)
        pick = jnp.concatenate([choose(at, half) for at in positions], axis=0)
        irr_row = jnp.sum(pick * irr_f, axis=1, keepdims=True).astype(jnp.int32)
        pick = pick.astype(BF16)
        near = lax.dot_general(
            pick, counts, (((1,), (1,)), ((), ())), preferred_element_type=F32
        )
        kind = jnp.bitwise_xor(irr_row, irr)
        weights = jnp.concatenate(
            [jnp.where(kind == q, near, 0.0).astype(BF16) for q in range(8)], axis=0
        )
        grouped = jnp.dot(weights, c_ref[...], preferred_element_type=F32).astype(BF16)
        for q in range(8):
            for u in range(n):
                for a in range(4):
                    g_ref[u * 128 + a * 32 : u * 128 + (a + 1) * 32, q * 128 : (q + 1) * 128] = (
                        grouped[q * n * 32 + u * 32 : q * n * 32 + (u + 1) * 32, a * 128 : (a + 1) * 128]
                    )
        mixed = jnp.dot(
            g_ref[: n * 128, :], b_ref[:, :cols], preferred_element_type=F32
        ).astype(BF16)
        for u in range(n):
            z_ref[0:128, u * 128 : (u + 1) * 128] = mixed[u * 128 : (u + 1) * 128, 0:128]
            z_ref[128:256, u * 128 : (u + 1) * 128] = mixed[u * 128 : (u + 1) * 128, 128:256]
        return pick, mixed

    def pack(width):
        rows = jnp.dot(msg_ref[...], z_ref[:, :width], preferred_element_type=F32)
        return rows.reshape(32, 8, width).astype(BF16)

    def chunk_a(half):
        units(peers, half, 256)
        rows = pack(384)
        send_a[half * 32 : (half + 1) * 32] = rows[:, :, :128]
        send_c[half * 32 : (half + 1) * 32] = rows[:, :, 128:]

    def chunk_b(half):
        pick, mixed = units([ib], half, 384)
        own = jnp.dot(pick, c_ref[...], preferred_element_type=F32).astype(BF16)
        for a in range(4):
            z_ref[a * 32 : (a + 1) * 32, 128:256] = own[:, a * 128 : (a + 1) * 128]
        z_ref[128:256, 128:256] = mixed[:, 256:384]
        send_b[half * 32 : (half + 1) * 32] = pack(256)

    sends = ((send_a, recv_a), (send_c, recv_c), (send_b, recv_b))

    def send(which, z_to):
        src, dst = sends[which]

        def one(k, carry):
            y_to, core_to = k // 2, (core + k) % 2
            to = place(y_to, z_to, core_to)

            @pl.when(to != me)
            def _():
                pltpu.make_async_remote_copy(
                    src_ref=src.at[(z_to // 4) * 32 + y_to * 8 + (z_to % 4) * 2 + core_to],
                    dst_ref=dst.at[me],
                    send_sem=str_send.at[which],
                    recv_sem=str_recv.at[which],
                    device_id=(to, ib),
                    device_id_type=MESH,
                ).start()

            return carry

        lax.fori_loop(0, 8, one, 0)

    def send_some(which, owners):
        src, dst = sends[which]
        for z_to, y_to in owners:
            for k in range(2):
                core_to = (core + k) % 2
                to = place(y_to, z_to, core_to)

                @pl.when(to != me)
                def _():
                    pltpu.make_async_remote_copy(
                        src_ref=src.at[(z_to // 4) * 32 + y_to * 8 + (z_to % 4) * 2 + core_to],
                        dst_ref=dst.at[me],
                        send_sem=str_send.at[which],
                        recv_sem=str_recv.at[which],
                        device_id=(to, ib),
                        device_id_type=MESH,
                    ).start()

    def await_all(ref, sem):
        some = ref.at[pl.ds(0, n_str - 1)]
        pltpu.make_async_copy(some, some, sem).wait()

    chunk_a(0)
    pl.semaphore_wait(barrier, 63 + n_ib - 1)
    for z_to in NEAR:
        send(0, z_to)
    chunk_a(1)
    for z_to in FAR:
        send(0, z_to)
    for z_to in NEAR:
        send(1, z_to)
    chunk_b(0)
    for z_to in FAR[:2]:
        send(1, z_to)
    chunk_b(1)
    for z_to in FAR[2:]:
        send(1, z_to)
    send_some(2, NEAR_LAST)
    send_some(2, FAR_LAST)

    mine = (z // 4) * 32 + y * 8 + (z % 4) * 2 + core
    recv_a[me] = send_a[mine]
    recv_c[me] = send_c[mine]
    def received(ref):
        return ref[...].reshape(512, ref.shape[2])

    def to_peer(u):
        slot = jnp.where(ib < peers[u], ib, ib - 1)
        return pltpu.make_async_remote_copy(
            src_ref=part_s.at[u],
            dst_ref=part_r.at[slot],
            send_sem=ib_send.at[u],
            recv_sem=ib_recv.at[slot],
            device_id=(me, peers[u]),
            device_id_type=MESH,
        )

    def first_peer():
        await_all(recv_a, str_recv.at[0])
        part_s[0] = jnp.dot(
            alpha_ref[...], received(recv_a), preferred_element_type=F32
        ).astype(BF16)
        to_peer(0).start()

    recv_b[me] = send_b[mine]
    r = iota((512, 512), 0)
    c = iota((512, 512), 1)
    from_cols = jnp.where(
        r == (c // 4 % 2) * 256 + (c // 8) * 4 + c % 4, 1.0, 0.0
    ).astype(BF16)
    for load in loads[8:]:
        load.wait()
    alpha_ref[...] = jnp.dot(a_ref[...], from_cols, preferred_element_type=F32).astype(BF16)
    eye = jnp.where(iota((256, 256), 0) == iota((256, 256), 1), 1.0, 0.0).astype(BF16)
    same = jnp.concatenate([as_ref[...], eye], axis=1)
    same_ref[...] = jnp.dot(same, from_cols, preferred_element_type=F32).astype(BF16)

    first_peer()
    await_all(recv_c, str_recv.at[1])
    partial = jnp.dot(alpha_ref[...], received(recv_c), preferred_element_type=F32).astype(BF16)
    for u in (1, 2):
        part_s[u] = partial[:, (u - 1) * 128 : u * 128]
        to_peer(u).start()
    await_all(recv_b, str_recv.at[2])
    x = received(recv_b)
    total = jnp.dot(alpha_ref[...], x[:, 0:128], preferred_element_type=F32) + jnp.dot(
        same_ref[...], x[:, 128:256], preferred_element_type=F32
    )
    for k in range(3):
        pltpu.make_async_copy(part_r.at[k], part_r.at[k], ib_recv.at[k]).wait()
        total = total + part_r[k].astype(F32)
    out_ref[...] = total.astype(BF16)
    for u in range(3):
        to_peer(u).wait_send()
    await_all(send_a, str_send.at[0])
    await_all(send_c, str_send.at[1])
    await_all(send_b, str_send.at[2])


def local(
    n_str,
    n_ib,
    coeffs,
    block_irrep,
    couple_block,
    couple_sign,
    block_order,
    alpha_same,
    alpha_mixed,
    beta_same,
    beta_mixed,
):
    hbm = pl.BlockSpec(memory_space=pltpu.HBM)
    return pl.pallas_call(
        functools.partial(kernel, n_str, n_ib),
        out_shape=pltpu.VMEM((256, 128), BF16),
        in_specs=[hbm] * 9,
        out_specs=pl.BlockSpec(memory_space=pltpu.VMEM),
        scratch_shapes=[
            pltpu.VMEM((256, 4, 128), BF16),
            pltpu.VMEM((256, 4, 128), F32),
            pltpu.VMEM((256, 512), BF16),
            pltpu.VMEM((1, 256), jnp.int32),
            pltpu.VMEM((8, 256), jnp.int32),
            pltpu.VMEM((8, 256), jnp.int32),
            pltpu.VMEM((1, 256), jnp.int32),
            pltpu.VMEM((1024, 384), BF16),
            pltpu.VMEM((256, 512), BF16),
            pltpu.VMEM((256, 256), BF16),
            pltpu.VMEM((256, 256), BF16),
            pltpu.VMEM((256, 512), BF16),
            pltpu.VMEM((256, 512), BF16),
            pltpu.VMEM((384, 1024), BF16),
            pltpu.VMEM((256, 384), BF16),
            pltpu.VMEM((64, 8, 128), BF16),
            pltpu.VMEM((64, 8, 256), BF16),
            pltpu.VMEM((64, 8, 256), BF16),
            pltpu.VMEM((64, 8, 128), BF16),
            pltpu.VMEM((64, 8, 256), BF16),
            pltpu.VMEM((64, 8, 256), BF16),
            pltpu.VMEM((3, 256, 128), BF16),
            pltpu.VMEM((3, 256, 128), BF16),
            pltpu.SemaphoreType.DMA((11,)),
            pltpu.SemaphoreType.DMA((3,)),
            pltpu.SemaphoreType.DMA((3,)),
            pltpu.SemaphoreType.DMA((3,)),
            pltpu.SemaphoreType.DMA((3,)),
            pltpu.SemaphoreType.REGULAR,
            pltpu.SemaphoreType.REGULAR,
            pltpu.SemaphoreType.REGULAR,
        ],
        compiler_params=pltpu.CompilerParams(
            collective_id=0, has_side_effects=True, vmem_limit_bytes=62 * 1024 * 1024
        ),
    )(
        coeffs.reshape(4, 256, 128).transpose(1, 0, 2),
        block_irrep.reshape(1, 256),
        couple_block.T,
        couple_sign.T,
        block_order.reshape(1, 256),
        alpha_same,
        alpha_mixed,
        beta_same.reshape(1024, 128),
        beta_mixed.reshape(2, 1024, 128),
    )


def solution(mesh):
    in_specs = (
        P("str", None),
        P(),
        P(),
        P(),
        P(),
        P(),
        P("ib", None, None),
        P(),
        P("ib", None, None, None),
    )
    body = functools.partial(local, mesh.shape["str"], mesh.shape["ib"])
    return jax.shard_map(
        body, mesh=mesh, in_specs=in_specs, out_specs=P(None, ("str", "ib")), check_vma=False
    )
```

```python
import functools

import jax
import jax.numpy as jnp
from jax import lax
from jax.experimental import pallas as pl
from jax.experimental.pallas import tpu as pltpu
from jax.sharding import PartitionSpec as P

MESH = pl.DeviceIdType.MESH
F32 = jnp.float32
BF16 = jnp.bfloat16
FAR = (4, 7, 5, 6)
NEAR = ((0, 0), (0, 1), (1, 0), (0, 2), (1, 1), (0, 3), (2, 0), (1, 2), (2, 1), (1, 3), (3, 0), (2, 2), (3, 1), (2, 3), (3, 2), (3, 3))
FAR_LAST = ((4, 0), (5, 0), (6, 0), (7, 0), (4, 1), (4, 2), (4, 3), (5, 1), (5, 2), (5, 3), (6, 1), (6, 2), (6, 3), (7, 1), (7, 2), (7, 3))


def iota(shape, dim):
    return lax.broadcasted_iota(jnp.int32, shape, dim)


def kernel(
    n_str,
    n_ib,
    coef_hbm,
    irr_hbm,
    cb_hbm,
    sg_hbm,
    ord_hbm,
    as_hbm,
    am_hbm,
    bs_hbm,
    bm_hbm,
    out_ref,
    coef_ref,
    coef_f,
    c_ref,
    irr_ref,
    cb_ref,
    sg_ref,
    ord_ref,
    b_ref,
    a_ref,
    as_ref,
    msg_ref,
    alpha_ref,
    same_ref,
    g_ref,
    z_ref,
    send_a,
    send_c,
    send_b,
    recv_a,
    recv_c,
    recv_b,
    part_s,
    part_r,
    load_sem,
    str_send,
    str_recv,
    ib_send,
    ib_recv,
    late_sem,
    plane_sem,
    all_sem,
):
    me = lax.axis_index("str")
    ib = lax.axis_index("ib")

    loads = [
        pltpu.make_async_copy(cb_hbm, cb_ref, load_sem.at[0]),
        pltpu.make_async_copy(sg_hbm, sg_ref, load_sem.at[1]),
        pltpu.make_async_copy(irr_hbm, irr_ref, load_sem.at[2]),
        pltpu.make_async_copy(ord_hbm, ord_ref, load_sem.at[3]),
        pltpu.make_async_copy(coef_hbm, coef_ref, load_sem.at[4]),
        pltpu.make_async_copy(bm_hbm.at[0], b_ref.at[:, pl.ds(0, 128)], load_sem.at[5]),
        pltpu.make_async_copy(bm_hbm.at[1], b_ref.at[:, pl.ds(128, 128)], load_sem.at[6]),
        pltpu.make_async_copy(bs_hbm, b_ref.at[:, pl.ds(256, 128)], load_sem.at[7]),
        pltpu.make_async_copy(am_hbm.at[0], a_ref.at[:, pl.ds(0, 256)], load_sem.at[8]),
        pltpu.make_async_copy(am_hbm.at[1], a_ref.at[:, pl.ds(256, 256)], load_sem.at[9]),
        pltpu.make_async_copy(as_hbm, as_ref, load_sem.at[10]),
    ]
    for load in loads:
        load.start()

    y, z, core = me // 16, (me // 2) % 8, me % 2

    def place(y_to, z_to, core_to):
        return (((y_to % 4) * 8) + (z_to % 8)) * 2 + core_to % 2

    barrier = pltpu.get_barrier_semaphore()

    for k in range(1, n_ib):
        pl.semaphore_signal(
            barrier, inc=1, device_id=(me, lax.rem(ib + k, n_ib)), device_id_type=MESH
        )

    for k in range(1, 64):
        pl.semaphore_signal(
            barrier, inc=1, device_id=((me + k) % 64, ib), device_id_type=MESH
        )

    r = iota((256, 256), 0)
    c = iota((256, 256), 1)
    msg_ref[...] = jnp.where(
        c == (r // 4 % 2) * 128 + (r % 4) * 32 + r // 8, 1.0, 0.0
    ).astype(BF16)
    lane = iota((32, 256), 1)
    sub = iota((32, 256), 0)
    lane_f = lane.astype(F32)
    row = iota((256, 256), 0)

    for load in loads[:4]:
        load.wait()
    cb = cb_ref[...]
    sg = sg_ref[...]
    counts = jnp.zeros((256, 256), jnp.int32)
    for k in range(8):
        counts = counts + jnp.where(row == cb[k : k + 1, :], sg[k : k + 1, :], 0)
    counts = counts.astype(F32).astype(BF16)
    irr = irr_ref[...]
    irr_f = irr.astype(F32)
    order_f = ord_ref[...].astype(F32)

    loads[4].wait()
    coef_f[...] = coef_ref[...].astype(F32)
    for a in range(4):
        c_ref[:, a * 128 : (a + 1) * 128] = coef_f[:, a, :].astype(BF16)
    for load in loads[5:8]:
        load.wait()

    peers = [jnp.where(ib > u, u, u + 1) for u in range(3)]

    def choose(position, half):
        owner = (sub // 8) * 16 + (4 * half + sub // 2 % 4) * 2 + sub % 2
        owned = jnp.sum(
            jnp.where(lane == 4 * owner + position, order_f, 0.0), axis=1, keepdims=True
        )
        return jnp.where(lane_f == owned, 1.0, 0.0)

    def units(positions, half, cols):
        n = len(positions)
        pick = jnp.concatenate([choose(at, half) for at in positions], axis=0)
        irr_row = jnp.sum(pick * irr_f, axis=1, keepdims=True).astype(jnp.int32)
        pick = pick.astype(BF16)
        near = lax.dot_general(
            pick, counts, (((1,), (1,)), ((), ())), preferred_element_type=F32
        )
        kind = jnp.bitwise_xor(irr_row, irr)
        weights = jnp.concatenate(
            [jnp.where(kind == q, near, 0.0).astype(BF16) for q in range(8)], axis=0
        )
        grouped = jnp.dot(weights, c_ref[...], preferred_element_type=F32).astype(BF16)
        for q in range(8):
            for u in range(n):
                for a in range(4):
                    g_ref[u * 128 + a * 32 : u * 128 + (a + 1) * 32, q * 128 : (q + 1) * 128] = (
                        grouped[q * n * 32 + u * 32 : q * n * 32 + (u + 1) * 32, a * 128 : (a + 1) * 128]
                    )
        mixed = jnp.dot(
            g_ref[: n * 128, :], b_ref[:, :cols], preferred_element_type=F32
        ).astype(BF16)
        for u in range(n):
            z_ref[0:128, u * 128 : (u + 1) * 128] = mixed[u * 128 : (u + 1) * 128, 0:128]
            z_ref[128:256, u * 128 : (u + 1) * 128] = mixed[u * 128 : (u + 1) * 128, 128:256]
        return pick, mixed

    def pack(width):
        rows = jnp.dot(msg_ref[...], z_ref[:, :width], preferred_element_type=F32)
        return rows.reshape(32, 8, width).astype(BF16)

    def chunk_a(half):
        units(peers, half, 256)
        rows = pack(384)
        send_a[half * 32 : (half + 1) * 32] = rows[:, :, :128]
        send_c[half * 32 : (half + 1) * 32] = rows[:, :, 128:]

    def chunk_b(half):
        pick, mixed = units([ib], half, 384)
        own = jnp.dot(pick, c_ref[...], preferred_element_type=F32).astype(BF16)
        for a in range(4):
            z_ref[a * 32 : (a + 1) * 32, 128:256] = own[:, a * 128 : (a + 1) * 128]
        z_ref[128:256, 128:256] = mixed[:, 256:384]
        send_b[half * 32 : (half + 1) * 32] = pack(256)

    sends = ((send_a, recv_a), (send_c, recv_c), (send_b, recv_b))

    def send(which, z_to):
        src, dst = sends[which]

        def one(k, carry):
            y_to, core_to = k // 2, (core + k) % 2
            to = place(y_to, z_to, core_to)

            @pl.when(to != me)
            def _():
                pltpu.make_async_remote_copy(
                    src_ref=src.at[(z_to // 4) * 32 + y_to * 8 + (z_to % 4) * 2 + core_to],
                    dst_ref=dst.at[me],
                    send_sem=str_send.at[which],
                    recv_sem=str_recv.at[which],
                    device_id=(to, ib),
                    device_id_type=MESH,
                ).start()

            return carry

        lax.fori_loop(0, 8, one, 0)

    def send_some(which, owners):
        src, dst = sends[which]
        for z_to, y_to in owners:
            for k in range(2):
                core_to = (core + k) % 2
                to = place(y_to, z_to, core_to)

                @pl.when(to != me)
                def _():
                    pltpu.make_async_remote_copy(
                        src_ref=src.at[(z_to // 4) * 32 + y_to * 8 + (z_to % 4) * 2 + core_to],
                        dst_ref=dst.at[me],
                        send_sem=str_send.at[which],
                        recv_sem=str_recv.at[which],
                        device_id=(to, ib),
                        device_id_type=MESH,
                    ).start()

    def await_all(ref, sem):
        some = ref.at[pl.ds(0, n_str - 1)]
        pltpu.make_async_copy(some, some, sem).wait()

    chunk_a(0)
    pl.semaphore_wait(barrier, 63 + n_ib - 1)
    send_some(0, NEAR)
    chunk_a(1)
    for z_to in FAR:
        send(0, z_to)
    send_some(1, NEAR)
    chunk_b(0)
    for z_to in FAR[:2]:
        send(1, z_to)
    chunk_b(1)
    for z_to in FAR[2:]:
        send(1, z_to)
    send_some(2, NEAR)
    send_some(2, FAR_LAST)

    mine = (z // 4) * 32 + y * 8 + (z % 4) * 2 + core
    recv_a[me] = send_a[mine]
    recv_c[me] = send_c[mine]
    def received(ref):
        return ref[...].reshape(512, ref.shape[2])

    def to_peer(u):
        slot = jnp.where(ib < peers[u], ib, ib - 1)
        return pltpu.make_async_remote_copy(
            src_ref=part_s.at[u],
            dst_ref=part_r.at[slot],
            send_sem=ib_send.at[u],
            recv_sem=ib_recv.at[slot],
            device_id=(me, peers[u]),
            device_id_type=MESH,
        )

    def first_peer():
        await_all(recv_a, str_recv.at[0])
        part_s[0] = jnp.dot(
            alpha_ref[...], received(recv_a), preferred_element_type=F32
        ).astype(BF16)
        to_peer(0).start()

    recv_b[me] = send_b[mine]
    r = iota((512, 512), 0)
    c = iota((512, 512), 1)
    from_cols = jnp.where(
        r == (c // 4 % 2) * 256 + (c // 8) * 4 + c % 4, 1.0, 0.0
    ).astype(BF16)
    for load in loads[8:]:
        load.wait()
    alpha_ref[...] = jnp.dot(a_ref[...], from_cols, preferred_element_type=F32).astype(BF16)
    eye = jnp.where(iota((256, 256), 0) == iota((256, 256), 1), 1.0, 0.0).astype(BF16)
    same = jnp.concatenate([as_ref[...], eye], axis=1)
    same_ref[...] = jnp.dot(same, from_cols, preferred_element_type=F32).astype(BF16)

    first_peer()
    await_all(recv_c, str_recv.at[1])
    partial = jnp.dot(alpha_ref[...], received(recv_c), preferred_element_type=F32).astype(BF16)
    for u in (1, 2):
        part_s[u] = partial[:, (u - 1) * 128 : u * 128]
        to_peer(u).start()
    await_all(recv_b, str_recv.at[2])
    x = received(recv_b)
    total = jnp.dot(alpha_ref[...], x[:, 0:128], preferred_element_type=F32) + jnp.dot(
        same_ref[...], x[:, 128:256], preferred_element_type=F32
    )
    for k in range(3):
        pltpu.make_async_copy(part_r.at[k], part_r.at[k], ib_recv.at[k]).wait()
        total = total + part_r[k].astype(F32)
    out_ref[...] = total.astype(BF16)
    for u in range(3):
        to_peer(u).wait_send()
    await_all(send_a, str_send.at[0])
    await_all(send_c, str_send.at[1])
    await_all(send_b, str_send.at[2])


def local(
    n_str,
    n_ib,
    coeffs,
    block_irrep,
    couple_block,
    couple_sign,
    block_order,
    alpha_same,
    alpha_mixed,
    beta_same,
    beta_mixed,
):
    hbm = pl.BlockSpec(memory_space=pltpu.HBM)
    return pl.pallas_call(
        functools.partial(kernel, n_str, n_ib),
        out_shape=pltpu.VMEM((256, 128), BF16),
        in_specs=[hbm] * 9,
        out_specs=pl.BlockSpec(memory_space=pltpu.VMEM),
        scratch_shapes=[
            pltpu.VMEM((256, 4, 128), BF16),
            pltpu.VMEM((256, 4, 128), F32),
            pltpu.VMEM((256, 512), BF16),
            pltpu.VMEM((1, 256), jnp.int32),
            pltpu.VMEM((8, 256), jnp.int32),
            pltpu.VMEM((8, 256), jnp.int32),
            pltpu.VMEM((1, 256), jnp.int32),
            pltpu.VMEM((1024, 384), BF16),
            pltpu.VMEM((256, 512), BF16),
            pltpu.VMEM((256, 256), BF16),
            pltpu.VMEM((256, 256), BF16),
            pltpu.VMEM((256, 512), BF16),
            pltpu.VMEM((256, 512), BF16),
            pltpu.VMEM((384, 1024), BF16),
            pltpu.VMEM((256, 384), BF16),
            pltpu.VMEM((64, 8, 128), BF16),
            pltpu.VMEM((64, 8, 256), BF16),
            pltpu.VMEM((64, 8, 256), BF16),
            pltpu.VMEM((64, 8, 128), BF16),
            pltpu.VMEM((64, 8, 256), BF16),
            pltpu.VMEM((64, 8, 256), BF16),
            pltpu.VMEM((3, 256, 128), BF16),
            pltpu.VMEM((3, 256, 128), BF16),
            pltpu.SemaphoreType.DMA((11,)),
            pltpu.SemaphoreType.DMA((3,)),
            pltpu.SemaphoreType.DMA((3,)),
            pltpu.SemaphoreType.DMA((3,)),
            pltpu.SemaphoreType.DMA((3,)),
            pltpu.SemaphoreType.REGULAR,
            pltpu.SemaphoreType.REGULAR,
            pltpu.SemaphoreType.REGULAR,
        ],
        compiler_params=pltpu.CompilerParams(
            collective_id=0, has_side_effects=True, vmem_limit_bytes=62 * 1024 * 1024
        ),
    )(
        coeffs.reshape(4, 256, 128).transpose(1, 0, 2),
        block_irrep.reshape(1, 256),
        couple_block.T,
        couple_sign.T,
        block_order.reshape(1, 256),
        alpha_same,
        alpha_mixed,
        beta_same.reshape(1024, 128),
        beta_mixed.reshape(2, 1024, 128),
    )


def solution(mesh):
    in_specs = (
        P("str", None),
        P(),
        P(),
        P(),
        P(),
        P(),
        P("ib", None, None),
        P(),
        P("ib", None, None, None),
    )
    body = functools.partial(local, mesh.shape["str"], mesh.shape["ib"])
    return jax.shard_map(
        body, mesh=mesh, in_specs=in_specs, out_specs=P(None, ("str", "ib")), check_vma=False
    )
```
